32 devices in a mesh: lon: 8 (over y, x, core), lat: 4 (over z).
Axes of the slice: x: 2, y: 2, z: 4, core: 2. Of those that a mesh axis runs over, the one named last changes fastest.
Arguments:
- fields: bfloat16 [4, 192, 896, 80], P(None, 'lat', 'lon'), may hold values from -6 to 6
- lift_weight: bfloat16 [80, 128], replicated, may hold values from -0.625 to 0.625
- near_kernel: bfloat16 [3, 3, 128, 128], replicated, may hold values from -0.1875 to 0.1875
- far_kernel: bfloat16 [3, 3, 128, 128], replicated, may hold values from -0.1875 to 0.1875
- mix_weight: bfloat16 [128, 128], replicated, may hold values from -0.5 to 0.5
Outputs:
- result: bfloat16 [4, 192, 896, 128], P(None, 'lat', 'lon')
The draws below stay inside these ranges and needn't reach their ends.
All inputs are finite; a program needn't handle non-finite values.
Results may differ from the reference program's by a relative error of at most 0.0067.
Values may be sent and summed in bfloat16 or wider, within the bound.
No kernel may reach another device: no remote copies, remote signals or barrier semaphores. Data moves between devices by JAX's collectives and lax.ppermute only.
A program may use at most 256 MiB of HBM per device.

```python
import jax
import jax.numpy as jnp
from jax import lax

C = 128
CIN = 80
BATCH = 4
CLAT = 48
FAR = 4
NLAT = 192
NLON = 896


def steps_of(rng, extent, cuts, low, high):
    def one(dim, shards_of):
        steps = jax.random.uniform(jax.random.fold_in(jax.random.fold_in(rng, 6), dim), (shards_of,), jnp.float32, low / len(cuts), high / len(cuts))
        return jnp.repeat(jnp.exp(steps), extent[dim] // shards_of).reshape((-1,) + (1,) * (len(extent) - dim - 1))

    factor_of = one(*cuts[0])
    for cut in cuts[1:]:
        factor_of = factor_of * one(*cut)
    return factor_of


def noise(own_key, dims, scale, most, shards=(), kind=jnp.bfloat16):
    drawn = jax.random.normal(own_key, dims, jnp.float32) * scale
    if len(shards) > 0:
        drawn = steps_of(own_key, dims, shards, -0.22, 0.18) * drawn
    return jnp.clip(drawn, min=-most, max=most).astype(kind)


def setup_inputs(seed: int = 0) -> dict:
    key_list = jax.random.split(jax.random.key(seed), 6)
    return {
        "fields": noise(key_list[0], (BATCH, NLAT, NLON, CIN), 1.0, 6.0, ((1, 4), (2, 8))),
        "lift_weight": noise(key_list[1], (CIN, C), CIN ** -0.5, 0.625),
        "near_kernel": noise(key_list[2], (3, 3, C, C), (9 * C) ** -0.5, 0.1875),
        "far_kernel": noise(key_list[3], (3, 3, C, C), (9 * C) ** -0.5, 0.1875),
        "mix_weight": noise(key_list[4], (C, C), C ** -0.5, 0.5),
    }


def pad_globe(field, width):
    half = field.shape[2] // 2
    top = jnp.roll(field[:, :width][:, ::-1], half, axis=2)
    bottom = jnp.roll(field[:, -width:][:, ::-1], half, axis=2)
    tall = jnp.concatenate([top, field, bottom], axis=1)
    return jnp.concatenate([tall[:, :, -width:], tall, tall[:, :, :width]], axis=2)


def convolve_act(padded, kernel, step, rows, cols, block):
    count = rows // block
    batch = padded.shape[0]
    width = kernel.shape[3]

    def one_block(index):
        start = (index * block).astype(jnp.int32)
        window = lax.dynamic_slice_in_dim(padded, start, block + 2 * step, 1)
        total = jnp.zeros((batch, block, cols, width), jnp.float32)
        for row_tap in range(3):
            for col_tap in range(3):
                piece = window[:, row_tap * step:row_tap * step + block, col_tap * step:col_tap * step + cols]
                total = total + jnp.einsum("bhwc,cd->bhwd", piece.astype(jnp.float32), kernel[row_tap, col_tap].astype(jnp.float32))
        return jax.nn.silu(total).astype(jnp.bfloat16)

    blocks = lax.map(one_block, jnp.arange(count, dtype=jnp.int32))
    return jnp.transpose(blocks, (1, 0, 2, 3, 4)).reshape(batch, rows, cols, width)


def reference(fields, lift_weight, near_kernel, far_kernel, mix_weight):
    def one_sample(sample):
        source = sample[None]
        lifted = jnp.einsum("bhwc,cd->bhwd", source.astype(jnp.float32), lift_weight.astype(jnp.float32)).astype(jnp.bfloat16)
        first = convolve_act(pad_globe(lifted, 1), near_kernel, 1, NLAT, NLON, CLAT)
        second = convolve_act(pad_globe(first, FAR), far_kernel, FAR, NLAT, NLON, CLAT)
        mixed = jnp.einsum("bhwc,cd->bhwd", second.astype(jnp.float32), mix_weight.astype(jnp.float32))
        return mixed.astype(jnp.bfloat16)[0]

    return lax.map(one_sample, fields)
```

```python
import functools

import jax
import jax.numpy as jnp
from jax import lax
from jax.experimental import pallas as pl
from jax.experimental.pallas import tpu as pltpu
from jax.sharding import PartitionSpec as P

FAR = 4
BF = jnp.bfloat16
F32 = jnp.float32
HALO = 5
SLOT = 8
MIB = 1 << 20
INNER_MIB = 60
OUTER_MIB = 60


def dot(a, b):
    return jnp.dot(a, b, preferred_element_type=F32)


def silu_of_half(h):
    return h + h * jnp.tanh(h)


def with_columns(row, right, left):
    return jnp.concatenate([row, right, left], axis=1)


def slot(ref, lead, row):
    per = 128 // SLOT
    at = (row % per) * SLOT
    return ref[lead, row // per, :, at : at + SLOT]


def three_taps(row):
    before = jnp.concatenate([row[:, 127:], row[:, :127]], axis=1)
    after = jnp.concatenate([row[:, 1:], row[:, :1]], axis=1)
    fill = jnp.zeros((256 - 3 * row.shape[0], 128), BF)
    return jnp.concatenate([before, row, after, fill], axis=0).T


def pack_columns(x_ref, west_ref, east_ref):
    per = 128 // SLOT
    cols = x_ref.shape[3]
    for group in range(west_ref.shape[1]):
        rows = range(group * per, min((group + 1) * per, x_ref.shape[1]))
        west = [x_ref[0, r, :, 0:SLOT] for r in rows]
        east = [x_ref[0, r, :, cols - SLOT : cols] for r in rows]
        west_ref[0, group] = jnp.concatenate(west, axis=1)
        east_ref[0, group] = jnp.concatenate(east, axis=1)


def make_weights(lift_ref, near_ref, far_ref, mix_ref, wn_ref, wf_ref, wm_ref):
    cin, chan = lift_ref.shape
    wn_ref[...] = jnp.zeros_like(wn_ref)
    wf_ref[...] = jnp.zeros_like(wf_ref)
    wm_ref[...] = jnp.zeros_like(wm_ref)
    for a in range(3):
        for b in range(3):
            near = (0.5 * dot(lift_ref[...], near_ref[a, b])).astype(BF)
            far = (0.5 * far_ref[a, b].astype(F32)).astype(BF)
            for o in range(2):
                out = slice(o * chan, (o + 1) * chan)
                wn_ref[a + o, b * cin : (b + 1) * cin, out] = near
                k = a + o
                base = (2 * b + k // 2) * 256 + (k % 2) * chan
                wf_ref[base : base + chan, out] = far
    wm_ref[:chan, :chan] = mix_ref[...]
    wm_ref[chan:, chan:] = mix_ref[...]


def pack_rows(top_ref, bottom_ref, right_ref, left_ref, p_ref, q_ref):
    even = lax.rem(lax.axis_index("lat"), 2) == 0
    rows = right_ref.shape[1] * (128 // SLOT)
    batch = top_ref.shape[0]

    def write(first, second):
        for b in range(batch):
            for k in range(HALO):
                t = with_columns(top_ref[b, k], slot(right_ref, b, k), slot(left_ref, b, k))
                r = rows - HALO + k
                u = with_columns(
                    bottom_ref[b, 8 - HALO + k], slot(right_ref, b, r), slot(left_ref, b, r)
                )
                first[b, k] = t
                second[b, k] = u

    @pl.when(even)
    def _():
        write(p_ref, q_ref)

    @pl.when(jnp.logical_not(even))
    def _():
        write(q_ref, p_ref)


def spread(f2, at, piece):
    inner = f2.shape[-2]
    f2[(0, *at)] = jnp.concatenate([piece[128 - FAR :], piece[: inner - FAR]], axis=0)
    f2[(1, *at)] = piece[:inner]
    f2[(2, *at)] = piece[FAR : inner + FAR]


def near_block(rows, wn_ref):
    lhs = jnp.concatenate(
        [jnp.concatenate([pair[i] for pair in rows], axis=0) for i in range(4)], axis=1
    )
    h = dot(lhs, wn_ref[...].reshape(4 * 256, 256))
    return silu_of_half(h).astype(BF)


def far_block(f2, lead, g, wf_ref):
    lhs = jnp.concatenate(
        [
            jnp.concatenate([f2[(b, *lead, g + k, h, c)] for c in range(4)], axis=0)
            for b in range(3)
            for k in range(2)
            for h in range(2)
        ],
        axis=1,
    )
    return silu_of_half(dot(lhs, wf_ref[...])).astype(BF)


def halves(v, pair):
    return [v[128 * pair : 128 * pair + 128, 128 * o : 128 * o + 128] for o in range(2)]


def inner_rows(
    x_ref, right_ref, left_ref, lift_ref, near_ref, far_ref, mix_ref, out_ref, fx_ref,
    x3, f2, s, wn_ref, wf_ref, wm_ref,
):
    @pl.when(pl.program_id(0) == 0)
    def _():
        make_weights(lift_ref, near_ref, far_ref, mix_ref, wn_ref, wf_ref, wm_ref)

    blocks = f2.shape[1]
    cols = f2.shape[-2]
    low = FAR - 1
    for i in range(x3.shape[0]):
        r = i + low
        row = with_columns(x_ref[0, r], slot(right_ref, 0, r), slot(left_ref, 0, r))
        x3[i] = three_taps(row)
    for m in range(blocks):
        v = near_block(
            [[x3[8 * m + 2 * p + i] for i in range(4)] for p in range(4)], wn_ref
        )
        for p in range(4):
            for o, piece in enumerate(halves(v, p)):
                h, c = divmod(2 * p + o, 4)
                spread(f2, (m, h, c), piece)
                if m == 0:
                    fx_ref[0, 0, h, c] = piece
                if m == blocks - 1:
                    fx_ref[0, 1, h, c] = piece
    span = 4 * cols
    for g in range(blocks - 1):
        s[g * span : (g + 1) * span] = far_block(f2, (), g, wf_ref)
    y = dot(s[...], wm_ref[...]).astype(BF)
    for g in range(blocks - 1):
        for c in range(4):
            at = g * span + c * cols
            for h in range(2):
                out_ref[0, 8 * g + 4 * h + c] = y[at : at + cols, 128 * h : 128 * h + 128]


def outer_rows(
    top_ref, bottom_ref, right_ref, left_ref, p_ref, q_ref, fx_ref,
    lift_ref, near_ref, far_ref, mix_ref, _, out_ref,
    x3, f2, s, y, wn_ref, wf_ref, wm_ref, sems,
):
    make_weights(lift_ref, near_ref, far_ref, mix_ref, wn_ref, wf_ref, wm_ref)
    lat = lax.axis_index("lat")
    even = lax.rem(lat, 2) == 0
    poles = (lat == 0, lat == lax.axis_size("lat") - 1)
    cols = f2.shape[-2]
    total = right_ref.shape[1] * (128 // SLOT)
    span = 4 * cols
    units = [(b, side) for b in range(top_ref.shape[0]) for side in range(2)]
    for u, (b, side) in enumerate(units):
        pole = poles[side]
        moved = pole if side == 0 else jnp.logical_not(pole)
        from_p = even if side == 0 else jnp.logical_not(even)
        base = jnp.where(moved, 1, 0)
        close = jnp.where(moved, 0, HALO - 1)
        for k in range(HALO):
            taps = three_taps(jnp.where(from_p, p_ref[b, k], q_ref[b, k]))
            x3[u, base + k] = taps
        x3[u, 6 if side == 0 else 11] = x3[u, base + close]
        own = top_ref if side == 0 else bottom_ref
        for k in range(HALO):
            r = k if side == 0 else total - HALO + k
            t = k if side == 0 else 8 - HALO + k
            taps = three_taps(with_columns(own[b, t], slot(right_ref, b, r), slot(left_ref, b, r)))
            x3[u, (7 if side == 0 else 6) + k] = taps
            if k == (0 if side == 0 else HALO - 1):
                x3[u, jnp.where(moved, 0, HALO)] = taps
    for u, (b, side) in enumerate(units):
        pole = poles[side]
        v = near_block(
            [[x3[u, first + i] for i in range(4)] for first in (0, 2, 6, 8)], wn_ref
        )
        for q in range(2):
            for o, piece in enumerate(halves(v, q)):
                c = 2 * q + o
                spread(f2, (u, side, side, jnp.where(pole, 3 - c, c)), piece)
            for o, piece in enumerate(halves(v, 2 + q)):
                spread(f2, (u, side, 1 - side, 2 * q + o), piece)
        for h in range(2):
            for c in range(4):
                spread(f2, (u, 1 - side, h, c), fx_ref[b, side, h, c])
    for u in range(len(units)):
        s[u * span : (u + 1) * span] = far_block(f2, (u,), 0, wf_ref)
    copies = []
    for u, (b, side) in enumerate(units):
        done = dot(s[u * span : (u + 1) * span], wm_ref[...]).astype(BF)
        for c in range(4):
            for h in range(2):
                y[u, 4 * h + c] = done[cols * c : cols * c + cols, 128 * h : 128 * h + 128]
        to = out_ref.at[b, pl.ds(0 if side == 0 else total - 8, 8)]
        copy = pltpu.make_async_copy(y.at[u], to, sems.at[u])
        copy.start()
        copies.append(copy)
    for copy in copies:
        copy.wait()


def whole(shape):
    return pl.BlockSpec(shape, lambda *_: (0,) * len(shape))


def per_sample(shape):
    return pl.BlockSpec((1,) + shape[1:], lambda b, *_: (b,) + (0,) * (len(shape) - 1))


def params(mib):
    return pltpu.CompilerParams(vmem_limit_bytes=mib * MIB)


def cost(flops, nbytes):
    return pl.CostEstimate(flops=flops, bytes_accessed=nbytes, transcendentals=0)


def swaps(lats, lons, offset):
    half = lons // 2
    pairs = []
    for lat in range(lats):
        other = lat + (1 if (lat + offset) % 2 == 0 else -1)
        for lon in range(lons):
            if 0 <= other < lats:
                pairs.append((lon * lats + other, lon * lats + lat))
            else:
                pairs.append(((lon + half) % lons * lats + lat, lon * lats + lat))
    return pairs


def on_device(fields, lift_weight, near_kernel, far_kernel, mix_weight):
    batch, rows, cols, cin = fields.shape
    chan = mix_weight.shape[1]
    lats, lons = lax.axis_size("lat"), lax.axis_size("lon")
    x = jnp.transpose(fields, (0, 1, 3, 2))
    groups = rows * SLOT // 128
    edge = (batch, groups, cin, 128)
    west, east = pl.pallas_call(
        pack_columns,
        grid=(batch,),
        in_specs=[per_sample(x.shape)],
        out_specs=[per_sample(edge)] * 2,
        out_shape=[jax.ShapeDtypeStruct(edge, BF)] * 2,
        compiler_params=params(60),
        cost_estimate=cost(0, 4 * MIB),
        name="pack_columns",
    )(x)
    right = lax.ppermute(west, "lon", [((i + 1) % lons, i) for i in range(lons)])
    left = lax.ppermute(east, "lon", [((i - 1) % lons, i) for i in range(lons)])
    weights = (lift_weight, near_kernel, far_kernel, mix_weight)
    shapes = [(4, 256, 256), (6 * 256, 256), (256, 256)]
    strip = (batch, HALO, cin, 128)
    last = rows // 8 - 1
    p_send, q_send = pl.pallas_call(
        pack_rows,
        grid=(1,),
        in_specs=[
            pl.BlockSpec((batch, 8, cin, cols), lambda i: (0, 0, 0, 0)),
            pl.BlockSpec((batch, 8, cin, cols), lambda i: (0, last, 0, 0)),
            whole(edge),
            whole(edge),
        ],
        out_specs=[whole(strip)] * 2,
        out_shape=[jax.ShapeDtypeStruct(strip, BF)] * 2,
        compiler_params=params(60),
        cost_estimate=cost(0, 2 * MIB),
        name="pack_rows",
    )(x, x, right, left)
    p_got = lax.ppermute(p_send, ("lon", "lat"), swaps(lats, lons, 1))
    q_got = lax.ppermute(q_send, ("lon", "lat"), swaps(lats, lons, 0))

    blocks = (rows - 8) // 8
    inner = rows - 16
    fx = (batch, 2, 2, 4, 128, chan)
    made = [pltpu.VMEM(shape, BF) for shape in shapes]
    out, edges = pl.pallas_call(
        inner_rows,
        grid=(batch,),
        in_specs=[per_sample(x.shape), per_sample(edge), per_sample(edge)]
        + [whole(w.shape) for w in weights],
        out_specs=[
            pl.BlockSpec(
                (pl.Element(1), pl.Element(inner), pl.Element(cols), pl.Element(chan)),
                lambda b: (b, 8, 0, 0),
            ),
            per_sample(fx),
        ],
        out_shape=[
            jax.ShapeDtypeStruct((batch, rows, cols, chan), BF),
            jax.ShapeDtypeStruct(fx, BF),
        ],
        scratch_shapes=[
            pltpu.VMEM((8 * blocks + 2, 128, 256), BF),
            pltpu.VMEM((3, blocks, 2, 4, cols, chan), BF),
            pltpu.VMEM(((blocks - 1) * 4 * cols, 256), BF),
        ]
        + made,
        compiler_params=params(INNER_MIB),
        cost_estimate=cost(11 * 10**9, 12 * MIB),
        name="inner_rows",
    )(x, right, left, *weights)
    units = 2 * batch
    edge_rows = pl.BlockSpec((batch, 8, cin, cols), lambda i: (0, 0, 0, 0))
    last_rows = pl.BlockSpec((batch, 8, cin, cols), lambda i: (0, last, 0, 0))
    return pl.pallas_call(
        outer_rows,
        grid=(1,),
        in_specs=[edge_rows, last_rows, whole(edge), whole(edge), whole(strip), whole(strip)]
        + [whole(fx)]
        + [whole(w.shape) for w in weights]
        + [pl.BlockSpec(memory_space=pl.ANY)],
        out_specs=pl.BlockSpec(memory_space=pl.ANY),
        out_shape=jax.ShapeDtypeStruct((batch, rows, cols, chan), BF),
        scratch_shapes=[
            pltpu.VMEM((units, 12, 128, 256), BF),
            pltpu.VMEM((3, units, 2, 2, 4, cols, chan), BF),
            pltpu.VMEM((units * 4 * cols, 256), BF),
            pltpu.VMEM((units, 8, cols, chan), BF),
        ]
        + made
        + [pltpu.SemaphoreType.DMA((units,))],
        input_output_aliases={11: 0},
        compiler_params=params(OUTER_MIB),
        cost_estimate=cost(5 * 10**9, 6 * MIB),
        name="outer_rows",
    )(x, x, right, left, p_got, q_got, edges, *weights, out)


def solution(mesh):
    return jax.shard_map(
        on_device,
        mesh=mesh,
        in_specs=(P(None, "lat", "lon", None), P(), P(), P(), P()),
        out_specs=P(None, "lat", "lon", None),
        check_vma=False,
    )
```

```python
import functools

import jax
import jax.numpy as jnp
from jax import lax
from jax.experimental import pallas as pl
from jax.experimental.pallas import tpu as pltpu
from jax.sharding import PartitionSpec as P

FAR = 4
BF = jnp.bfloat16
F32 = jnp.float32
HALO = 5
SLOT = 8
MIB = 1 << 20
FIRST_MIB = 16
INNER_MIB = 24
OUTER_MIB = 34
PACK_MIB = 12


def dot(a, b):
    return jnp.dot(a, b, preferred_element_type=F32)


def silu_of_half(h):
    return h + h * jnp.tanh(h)


def turned(v, shift):
    shift %= 128
    if shift == 0:
        return v
    return jnp.concatenate([v[:, 128 - shift :], v[:, : 128 - shift]], axis=1)


def widened(row):
    return jnp.concatenate([row, jnp.zeros((row.shape[0], 128 - row.shape[1]), BF)], axis=1)


def with_columns(row, right_ref, left_ref, lead, r):
    per = 128 // SLOT
    cols = row.shape[1]
    at = (r % per) * SLOT
    right = turned(right_ref[lead, r // per], cols - at)
    left = turned(left_ref[lead, r // per], 128 - SLOT - at)
    return jnp.concatenate([row, right[:, cols : cols + SLOT], left[:, cols + SLOT :]], axis=1)


def three_taps(row):
    before = jnp.concatenate([row[:, 127:], row[:, :127]], axis=1)
    after = jnp.concatenate([row[:, 1:], row[:, :1]], axis=1)
    fill = jnp.zeros((256 - 3 * row.shape[0], 128), BF)
    return jnp.concatenate([before, row, after, fill], axis=0).T


def pack_columns(*refs):
    *x_refs, west_ref, east_ref = refs
    lane = lax.broadcasted_iota(jnp.int32, (west_ref.shape[2], 128), 1)
    for group, x_ref in enumerate(x_refs):
        cols = x_ref.shape[3]
        rows = [widened(x_ref[0, i]) for i in range(x_ref.shape[1])]
        for start, ref in ((0, west_ref), (cols - SLOT, east_ref)):
            moved = [turned(row, i * SLOT - start) for i, row in enumerate(rows)]
            packed = moved[0]
            for i, row in enumerate(moved):
                packed = jnp.where(lane < i * SLOT, packed, row)
            ref[0, group] = packed


def make_near(lift_ref, near_ref, wn_ref):
    cin, chan = lift_ref.shape
    wn_ref[...] = jnp.zeros_like(wn_ref)
    for a in range(3):
        for b in range(3):
            near = (0.5 * dot(lift_ref[...], near_ref[a, b])).astype(BF)
            for o in range(2):
                wn_ref[a + o, b * cin : (b + 1) * cin, o * chan : (o + 1) * chan] = near


def make_far(far_ref, mix_ref, wf_ref, wm_ref):
    chan = mix_ref.shape[0]
    wf_ref[...] = jnp.zeros_like(wf_ref)
    wm_ref[...] = jnp.zeros_like(wm_ref)
    for a in range(3):
        for b in range(3):
            far = (0.5 * far_ref[a, b].astype(F32)).astype(BF)
            for o in range(2):
                k = a + o
                base = (2 * b + k // 2) * 256 + (k % 2) * chan
                wf_ref[base : base + chan, o * chan : (o + 1) * chan] = far
    wm_ref[:chan, :chan] = mix_ref[...]
    wm_ref[chan:, chan:] = mix_ref[...]


def pack_rows(rows, top_ref, bottom_ref, right_ref, left_ref, p_ref, q_ref):
    even = lax.rem(lax.axis_index("lat"), 2) == 0
    top, bottom = [], []
    for k in range(HALO):
        top.append(with_columns(top_ref[0, k], right_ref, left_ref, 0, k))
        r = rows - HALO + k
        bottom.append(with_columns(bottom_ref[0, 8 - HALO + k], right_ref, left_ref, 0, r))
    for k in range(HALO):
        p_ref[0, k] = jnp.where(even, top[k], bottom[k])
        q_ref[0, k] = jnp.where(even, bottom[k], top[k])


def spread(f2, at, piece):
    inner = f2.shape[-2]
    f2[(0, *at)] = jnp.concatenate([piece[128 - FAR :], piece[: inner - FAR]], axis=0)
    f2[(1, *at)] = piece[:inner]
    f2[(2, *at)] = piece[FAR : inner + FAR]


def near_block(rows, wn_ref):
    lhs = jnp.concatenate(
        [jnp.concatenate([pair[i] for pair in rows], axis=0) for i in range(4)], axis=1
    )
    return silu_of_half(dot(lhs, wn_ref[...].reshape(4 * 256, 256)))


def far_block(f2, lead, g, wf_ref):
    lhs = jnp.concatenate(
        [
            jnp.concatenate([f2[(b, *lead, g + k, h, c)] for c in range(4)], axis=0)
            for b in range(3)
            for k in range(2)
            for h in range(2)
        ],
        axis=1,
    )
    return silu_of_half(dot(lhs, wf_ref[...])).astype(BF)


def halves(v, pair, height):
    base = height * pair
    return [v[base : base + height, 128 * o : 128 * o + 128] for o in range(2)]


def first_rows(x_ref, lift_ref, near_ref, first_ref, x3, wn_ref):
    @pl.when(pl.program_id(0) == 0)
    def _():
        make_near(lift_ref, near_ref, wn_ref)

    cols = x_ref.shape[3]
    for i in range(x3.shape[0]):
        x3[i] = three_taps(widened(x_ref[0, i + FAR - 1]))[:cols]
    for m in range(first_ref.shape[1]):
        rows = [[x3[8 * m + 2 * p + i] for i in range(4)] for p in range(4)]
        v = near_block(rows, wn_ref).astype(BF)
        for p in range(4):
            for o, piece in enumerate(halves(v, p, cols)):
                h, c = divmod(2 * p + o, 4)
                first_ref[0, m, h, c] = piece


def joined(main, strip):
    end = main.shape[0]
    head = jnp.concatenate([strip[14:15], main[:16].astype(F32)[1:]], axis=0)
    tail = jnp.concatenate([main[end - 16 :].astype(F32)[:15], strip[1:2]], axis=0)
    beyond = jnp.concatenate([strip[2:6], strip[2:10], strip[10:14]], axis=0)
    return jnp.concatenate(
        [head.astype(BF), main[16 : end - 16], tail.astype(BF), beyond.astype(BF)], axis=0
    )


def inner_rows(
    first_ref, west_ref, east_ref, right_ref, left_ref, lift_ref, near_ref, far_ref, mix_ref,
    out_ref, fx_ref, strips, f2, s, wn_ref, wf_ref, wm_ref,
):
    @pl.when(pl.program_id(0) == 0)
    def _():
        make_near(lift_ref, near_ref, wn_ref)
        make_far(far_ref, mix_ref, wf_ref, wm_ref)

    blocks = f2.shape[1]
    cols = f2.shape[-2]
    per = 128 // SLOT
    lane = lax.rem(lax.broadcasted_iota(jnp.int32, (lift_ref.shape[0], 128), 1), SLOT)
    for g in range(west_ref.shape[1]):
        right = jnp.where(lane < 2, turned(east_ref[0, g], -6), turned(right_ref[0, g], 2))
        left = jnp.where(lane < 6, turned(left_ref[0, g], -2), turned(west_ref[0, g], 6))
        right, left = three_taps(right), three_taps(left)
        for i in range(per):
            at = slice(SLOT * i, SLOT * i + SLOT)
            strips[per * g + i] = jnp.concatenate([right[at], left[at]], axis=0)
    low = FAR - 1
    pairs = 4 * blocks
    rows = [[strips[low + 2 * q + i] for i in range(4)] for q in range(pairs)]
    v = near_block(rows, wn_ref)
    for q in range(pairs):
        m, p = divmod(q, 4)
        for o, strip in enumerate(halves(v, q, 16)):
            h, c = divmod(2 * p + o, 4)
            piece = joined(first_ref[0, m, h, c], strip)
            spread(f2, (m, h, c), piece)
            if m == 0:
                fx_ref[0, 0, h, c] = piece
            if m == blocks - 1:
                fx_ref[0, 1, h, c] = piece
    span = 4 * cols
    for g in range(blocks - 1):
        s[g * span : (g + 1) * span] = far_block(f2, (), g, wf_ref)
    y = dot(s[...], wm_ref[...]).astype(BF)
    for g in range(blocks - 1):
        for c in range(4):
            at = g * span + c * cols
            for h in range(2):
                out_ref[0, 8 * g + 4 * h + c] = y[at : at + cols, 128 * h : 128 * h + 128]


def outer_rows(
    top_ref, bottom_ref, right_ref, left_ref, p_ref, q_ref, fx_ref,
    lift_ref, near_ref, far_ref, mix_ref, _, out_ref,
    x3, f2, s, y, wn_ref, wf_ref, wm_ref, sems,
):
    make_near(lift_ref, near_ref, wn_ref)
    make_far(far_ref, mix_ref, wf_ref, wm_ref)
    lat = lax.axis_index("lat")
    even = lax.rem(lat, 2) == 0
    poles = (lat == 0, lat == lax.axis_size("lat") - 1)
    cols = f2.shape[-2]
    total = out_ref.shape[1]
    span = 4 * cols
    units = [(b, side) for b in range(top_ref.shape[0]) for side in range(2)]
    for u, (b, side) in enumerate(units):
        pole = poles[side]
        moved = pole if side == 0 else jnp.logical_not(pole)
        from_p = even if side == 0 else jnp.logical_not(even)
        base = jnp.where(moved, 1, 0)
        close = jnp.where(moved, 0, HALO - 1)
        for k in range(HALO):
            taps = three_taps(jnp.where(from_p, p_ref[b, k], q_ref[b, k]))
            x3[u, base + k] = taps
        x3[u, 6 if side == 0 else 11] = x3[u, base + close]
        own = top_ref if side == 0 else bottom_ref
        for k in range(HALO):
            r = k if side == 0 else total - HALO + k
            t = k if side == 0 else 8 - HALO + k
            taps = three_taps(with_columns(own[b, t], right_ref, left_ref, b, r))
            x3[u, (7 if side == 0 else 6) + k] = taps
            if k == (0 if side == 0 else HALO - 1):
                x3[u, jnp.where(moved, 0, HALO)] = taps
    for u, (b, side) in enumerate(units):
        pole = poles[side]
        v = near_block(
            [[x3[u, first + i] for i in range(4)] for first in (0, 2, 6, 8)], wn_ref
        ).astype(BF)
        for q in range(2):
            for o, piece in enumerate(halves(v, q, 128)):
                c = 2 * q + o
                spread(f2, (u, side, side, jnp.where(pole, 3 - c, c)), piece)
            for o, piece in enumerate(halves(v, 2 + q, 128)):
                spread(f2, (u, side, 1 - side, 2 * q + o), piece)
        for h in range(2):
            for c in range(4):
                spread(f2, (u, 1 - side, h, c), fx_ref[b, side, h, c])
    for u in range(len(units)):
        s[u * span : (u + 1) * span] = far_block(f2, (u,), 0, wf_ref)
    copies = []
    for u, (b, side) in enumerate(units):
        done = dot(s[u * span : (u + 1) * span], wm_ref[...]).astype(BF)
        for c in range(4):
            for h in range(2):
                y[u, 4 * h + c] = done[cols * c : cols * c + cols, 128 * h : 128 * h + 128]
        to = out_ref.at[b, pl.ds(0 if side == 0 else total - 8, 8)]
        copy = pltpu.make_async_copy(y.at[u], to, sems.at[u])
        copy.start()
        copies.append(copy)
    for copy in copies:
        copy.wait()


def whole(shape):
    return pl.BlockSpec(shape, lambda *_: (0,) * len(shape))


def per_sample(shape):
    return pl.BlockSpec((1,) + shape[1:], lambda b, *_: (b,) + (0,) * (len(shape) - 1))


def params(mib):
    return pltpu.CompilerParams(vmem_limit_bytes=mib * MIB)


def cost(flops, nbytes):
    return pl.CostEstimate(flops=flops, bytes_accessed=nbytes, transcendentals=0)


def swaps(lats, lons, offset):
    half = lons // 2
    pairs = []
    for lat in range(lats):
        other = lat + (1 if (lat + offset) % 2 == 0 else -1)
        for lon in range(lons):
            if 0 <= other < lats:
                pairs.append((lon * lats + other, lon * lats + lat))
            else:
                pairs.append(((lon + half) % lons * lats + lat, lon * lats + lat))
    return pairs


def made_weights():
    return [pltpu.VMEM(shape, BF) for shape in ((4, 256, 256), (6 * 256, 256), (256, 256))]


def edge_shape(x):
    per = 128 // SLOT
    return (x.shape[0], -(-x.shape[1] // per), x.shape[2], 128)


def call_pack(x):
    edge = edge_shape(x)
    return pl.pallas_call(
        pack_columns,
        grid=(x.shape[0],),
        in_specs=[
            pl.BlockSpec(
                (1, 128 // SLOT, x.shape[2], x.shape[3]), functools.partial(lambda g, b: (b, g, 0, 0), g)
            )
            for g in range(edge[1])
        ],
        out_specs=[per_sample(edge)] * 2,
        out_shape=[jax.ShapeDtypeStruct(edge, BF)] * 2,
        compiler_params=params(PACK_MIB),
        cost_estimate=cost(0, 4 * MIB),
        name="pack_columns",
    )(*[x] * edge[1])


def call_first(x, weights):
    batch, rows, _, cols = x.shape
    chan = weights[-1].shape[1]
    first = (batch, rows // 8 - 1, 2, 4, cols, chan)
    return pl.pallas_call(
        first_rows,
        grid=(batch,),
        in_specs=[per_sample(x.shape)] + [whole(w.shape) for w in weights[:2]],
        out_specs=per_sample(first),
        out_shape=jax.ShapeDtypeStruct(first, BF),
        scratch_shapes=[pltpu.VMEM((rows - 6, cols, 256), BF), made_weights()[0]],
        compiler_params=params(FIRST_MIB),
        cost_estimate=cost(6 * 10**9, 9 * MIB),
        name="first_rows",
    )(x, *weights[:2])


def call_inner(first, west, east, right, left, weights, rows):
    batch, blocks, _, _, cols, chan = first.shape
    fx = (batch, 2, 2, 4, 128, chan)
    inner = rows - 16
    return pl.pallas_call(
        inner_rows,
        grid=(batch,),
        in_specs=[per_sample(first.shape)]
        + [per_sample(right.shape)] * 4
        + [whole(w.shape) for w in weights],
        out_specs=[
            pl.BlockSpec(
                (pl.Element(1), pl.Element(inner), pl.Element(cols), pl.Element(chan)),
                lambda b: (b, 8, 0, 0),
            ),
            per_sample(fx),
        ],
        out_shape=[
            jax.ShapeDtypeStruct((batch, rows, cols, chan), BF),
            jax.ShapeDtypeStruct(fx, BF),
        ],
        scratch_shapes=[
            pltpu.VMEM((rows, 16, 256), BF),
            pltpu.VMEM((3, blocks, 2, 4, cols, chan), BF),
            pltpu.VMEM(((blocks - 1) * 4 * cols, 256), BF),
        ]
        + made_weights(),
        compiler_params=params(INNER_MIB),
        cost_estimate=cost(7 * 10**9, 12 * MIB),
        name="inner_rows",
    )(first, west, east, right, left, *weights)


def on_device(fields, lift_weight, near_kernel, far_kernel, mix_weight):
    batch, rows, cols, cin = fields.shape
    chan = mix_weight.shape[1]
    lats, lons = lax.axis_size("lat"), lax.axis_size("lon")
    x = jnp.transpose(fields, (0, 1, 3, 2))
    edge = edge_shape(x)
    west, east = call_pack(x)
    right = lax.ppermute(west, "lon", [((i + 1) % lons, i) for i in range(lons)])
    left = lax.ppermute(east, "lon", [((i - 1) % lons, i) for i in range(lons)])
    weights = (lift_weight, near_kernel, far_kernel, mix_weight)
    first = call_first(x, weights)
    strip = (batch, HALO, cin, 128)
    last = rows // 8 - 1
    p_send, q_send = pl.pallas_call(
        functools.partial(pack_rows, rows),
        grid=(batch,),
        in_specs=[
            pl.BlockSpec((1, 8, cin, cols), lambda b: (b, 0, 0, 0)),
            pl.BlockSpec((1, 8, cin, cols), lambda b: (b, last, 0, 0)),
            per_sample(edge),
            per_sample(edge),
        ],
        out_specs=[per_sample(strip)] * 2,
        out_shape=[jax.ShapeDtypeStruct(strip, BF)] * 2,
        compiler_params=params(PACK_MIB),
        cost_estimate=cost(0, 2 * MIB),
        name="pack_rows",
    )(x, x, right, left)
    p_got = lax.ppermute(p_send, ("lon", "lat"), swaps(lats, lons, 1))
    q_got = lax.ppermute(q_send, ("lon", "lat"), swaps(lats, lons, 0))

    out, edges = call_inner(first, west, east, right, left, weights, rows)
    units = 2 * batch
    fx = edges.shape
    made = made_weights()
    edge_rows = pl.BlockSpec((batch, 8, cin, cols), lambda i: (0, 0, 0, 0))
    last_rows = pl.BlockSpec((batch, 8, cin, cols), lambda i: (0, last, 0, 0))
    return pl.pallas_call(
        outer_rows,
        grid=(1,),
        in_specs=[edge_rows, last_rows, whole(edge), whole(edge), whole(strip), whole(strip)]
        + [whole(fx)]
        + [whole(w.shape) for w in weights]
        + [pl.BlockSpec(memory_space=pl.ANY)],
        out_specs=pl.BlockSpec(memory_space=pl.ANY),
        out_shape=jax.ShapeDtypeStruct((batch, rows, cols, chan), BF),
        scratch_shapes=[
            pltpu.VMEM((units, 12, 128, 256), BF),
            pltpu.VMEM((3, units, 2, 2, 4, cols, chan), BF),
            pltpu.VMEM((units * 4 * cols, 256), BF),
            pltpu.VMEM((units, 8, cols, chan), BF),
        ]
        + made
        + [pltpu.SemaphoreType.DMA((units,))],
        input_output_aliases={11: 0},
        compiler_params=params(OUTER_MIB),
        cost_estimate=cost(5 * 10**9, 6 * MIB),
        name="outer_rows",
    )(x, x, right, left, p_got, q_got, edges, *weights, out)


def solution(mesh):
    return jax.shard_map(
        on_device,
        mesh=mesh,
        in_specs=(P(None, "lat", "lon", None), P(), P(), P(), P()),
        out_specs=P(None, "lat", "lon", None),
        check_vma=False,
    )
```

```python
import functools

import jax
import jax.numpy as jnp
from jax import lax
from jax.experimental import pallas as pl
from jax.experimental.pallas import tpu as pltpu
from jax.sharding import PartitionSpec as P

FAR = 4
BF = jnp.bfloat16
F32 = jnp.float32
HALO = 5
SLOT = 8
LAG = 1
MIB = 1 << 20
FIRST_MIB = 16
INNER_MIB = 24
OUTER_MIB = 34
PACK_MIB = 12


def dot(a, b):
    return jnp.dot(a, b, preferred_element_type=F32)


def silu_of_half(h):
    return h + h * jnp.tanh(h)


def turned(v, shift):
    shift %= 128
    if shift == 0:
        return v
    return jnp.concatenate([v[:, 128 - shift :], v[:, : 128 - shift]], axis=1)


def widened(row):
    return jnp.concatenate([row, jnp.zeros((row.shape[0], 128 - row.shape[1]), BF)], axis=1)


def with_columns(row, right_ref, left_ref, lead, r):
    per = 128 // SLOT
    cols = row.shape[1]
    at = (r % per) * SLOT
    right = turned(right_ref[lead, r // per], cols - at)
    left = turned(left_ref[lead, r // per], 128 - SLOT - at)
    return jnp.concatenate([row, right[:, cols : cols + SLOT], left[:, cols + SLOT :]], axis=1)


def three_taps(row):
    cin = row.shape[0]
    fill = jnp.zeros((256 - 3 * cin, 128), BF)
    tall = jnp.concatenate([row, row, row, fill], axis=0).T
    lane = lax.broadcasted_iota(jnp.int32, (128, 128), 1)
    low, high = tall[:, :128], tall[:, 128:]
    before = jnp.concatenate([low[127:], low[:127]], axis=0)
    after = jnp.concatenate([high[1:], high[:1]], axis=0)
    low = jnp.where(lane < cin, before, low)
    high = jnp.where(lane < 2 * cin - 128, high, after)
    return jnp.concatenate([low, high], axis=1)


def pack_columns(*refs):
    *x_refs, west_ref, east_ref = refs
    lane = lax.broadcasted_iota(jnp.int32, (west_ref.shape[2], 128), 1)
    for group, x_ref in enumerate(x_refs):
        cols = x_ref.shape[3]
        rows = [widened(x_ref[0, i]) for i in range(x_ref.shape[1])]
        moved = [turned(row, i * SLOT) for i, row in enumerate(rows)]
        offset = cols - SLOT
        west, east = moved[0], moved[0]
        for i, row in enumerate(moved):
            west = jnp.where(lane < i * SLOT, west, row)
            at = (i * SLOT + offset) % 128
            east = jnp.where((lane >= at) & (lane < at + SLOT), row, east)
        west_ref[0, group] = west
        east_ref[0, group] = turned(east, -offset)


def make_near(lift_ref, near_ref, wn_ref):
    cin, chan = lift_ref.shape
    wn_ref[...] = jnp.zeros_like(wn_ref)
    for a in range(3):
        for b in range(3):
            near = (0.5 * dot(lift_ref[...], near_ref[a, b])).astype(BF)
            for o in range(2):
                wn_ref[a + o, b * cin : (b + 1) * cin, o * chan : (o + 1) * chan] = near


def make_far(far_ref, mix_ref, wf_ref, wm_ref):
    chan = mix_ref.shape[0]
    wf_ref[...] = jnp.zeros_like(wf_ref)
    wm_ref[...] = jnp.zeros_like(wm_ref)
    for a in range(3):
        for b in range(3):
            far = (0.5 * far_ref[a, b].astype(F32)).astype(BF)
            for o in range(2):
                k = a + o
                base = (2 * b + k // 2) * 256 + (k % 2) * chan
                wf_ref[base : base + chan, o * chan : (o + 1) * chan] = far
    wm_ref[:chan, :chan] = mix_ref[...]
    wm_ref[chan:, chan:] = mix_ref[...]


def pack_rows(rows, top_ref, bottom_ref, right_ref, left_ref, p_ref, q_ref):
    even = lax.rem(lax.axis_index("lat"), 2) == 0
    top, bottom = [], []
    for k in range(HALO):
        top.append(with_columns(top_ref[0, k], right_ref, left_ref, 0, k))
        r = rows - HALO + k
        bottom.append(with_columns(bottom_ref[0, 8 - HALO + k], right_ref, left_ref, 0, r))
    for k in range(HALO):
        p_ref[0, k] = jnp.where(even, top[k], bottom[k])
        q_ref[0, k] = jnp.where(even, bottom[k], top[k])


def spread(f2, at, half, piece):
    inner = f2.shape[-2]
    at = (*at, slice(None), slice(half * 128, half * 128 + 128))
    f2[(0, *at)] = jnp.concatenate([piece[128 - FAR :], piece[: inner - FAR]], axis=0)
    f2[(1, *at)] = piece[:inner]
    f2[(2, *at)] = piece[FAR : inner + FAR]


def near_block(rows, wn_ref):
    lhs = jnp.concatenate(
        [jnp.concatenate([pair[i] for pair in rows], axis=0) for i in range(4)], axis=1
    )
    return silu_of_half(dot(lhs, wn_ref[...].reshape(4 * 256, 256)))


def far_block(upper, lower, wf_ref):
    lhs = jnp.concatenate(
        [
            jnp.concatenate([ref[(b, *at, c)] for c in range(4)], axis=0)
            for b in range(3)
            for ref, at in (upper, lower)
        ],
        axis=1,
    )
    return silu_of_half(dot(lhs, wf_ref[...])).astype(BF)


def halves(v, pair, height):
    base = height * pair
    return [v[base : base + height, 128 * o : 128 * o + 128] for o in range(2)]


def first_rows(x_ref, lift_ref, near_ref, first_ref, *scratch):
    *x3s, wn_ref = scratch

    @pl.when(pl.program_id(0) == 0)
    def _():
        make_near(lift_ref, near_ref, wn_ref)

    cols = x_ref.shape[3]
    blocks = first_ref.shape[1]

    def build(m):
        for i in range(2 if m else 0, 10):
            taps = three_taps(widened(x_ref[0, 8 * m + i + FAR - 1]))[:cols]
            x3s[m][i] = taps
            if i >= 8 and m + 1 < blocks:
                x3s[m + 1][i - 8] = taps

    def store(m, v):
        for p in range(4):
            for o, piece in enumerate(halves(v, p, cols)):
                h, c = divmod(2 * p + o, 4)
                first_ref[0, m, h, c] = piece

    build(0)
    for m in range(blocks):
        rows = [[x3s[m][2 * p + i] for i in range(4)] for p in range(4)]
        if m + 1 < blocks:
            build(m + 1)
        store(m, near_block(rows, wn_ref).astype(BF))


def joined(main, strip):
    end = main.shape[0]
    head = jnp.concatenate([strip[14:15], main[:16].astype(F32)[1:]], axis=0)
    tail = jnp.concatenate([main[end - 16 :].astype(F32)[:15], strip[1:2]], axis=0)
    beyond = jnp.concatenate([strip[2:6], strip[2:10], strip[10:14]], axis=0)
    return jnp.concatenate(
        [head.astype(BF), main[16 : end - 16], tail.astype(BF), beyond.astype(BF)], axis=0
    )


def inner_rows(
    first_ref, west_ref, east_ref, right_ref, left_ref, lift_ref, near_ref, far_ref, mix_ref,
    out_ref, fx_ref, strips, *scratch
):
    *f2s, s, wn_ref, wf_ref, wm_ref = scratch

    @pl.when(pl.program_id(0) == 0)
    def _():
        make_near(lift_ref, near_ref, wn_ref)
        make_far(far_ref, mix_ref, wf_ref, wm_ref)

    blocks = len(f2s)
    cols = f2s[0].shape[-2]
    per = 128 // SLOT
    lane = lax.rem(lax.broadcasted_iota(jnp.int32, (lift_ref.shape[0], 128), 1), SLOT)
    for g in range(west_ref.shape[1]):
        right = jnp.where(lane < 2, turned(east_ref[0, g], -6), turned(right_ref[0, g], 2))
        left = jnp.where(lane < 6, turned(left_ref[0, g], -2), turned(west_ref[0, g], 6))
        right, left = three_taps(right), three_taps(left)
        for i in range(per):
            at = slice(SLOT * i, SLOT * i + SLOT)
            strips[per * g + i] = jnp.concatenate([right[at], left[at]], axis=0)
    low = FAR - 1
    pairs = 4 * blocks
    rows = [[strips[low + 2 * q + i] for i in range(4)] for q in range(pairs)]
    v = near_block(rows, wn_ref)
    span = 4 * cols

    def far(g):
        s[g * span : (g + 1) * span] = far_block((f2s[g], ()), (f2s[g + 1], ()), wf_ref)

    for m in range(blocks):
        for p in range(4):
            for o, strip in enumerate(halves(v, 4 * m + p, 16)):
                h, c = divmod(2 * p + o, 4)
                piece = joined(first_ref[0, m, h, c], strip)
                spread(f2s[m], (c,), h, piece)
                if m == 0:
                    fx_ref[0, 0, h, c] = piece
                if m == blocks - 1:
                    fx_ref[0, 1, h, c] = piece
        if m >= LAG + 1:
            far(m - 1 - LAG)
    for g in range(blocks - 1 - LAG, blocks - 1):
        far(g)
    y = dot(s[...], wm_ref[...]).astype(BF)
    for g in range(blocks - 1):
        for c in range(4):
            at = g * span + c * cols
            for h in range(2):
                out_ref[0, 8 * g + 4 * h + c] = y[at : at + cols, 128 * h : 128 * h + 128]


def outer_rows(
    p_own_ref, q_own_ref, p_ref, q_ref, fx_ref,
    lift_ref, near_ref, far_ref, mix_ref, _, out_ref,
    x3, f2, s, y, wn_ref, wf_ref, wm_ref, sems,
):
    make_near(lift_ref, near_ref, wn_ref)
    make_far(far_ref, mix_ref, wf_ref, wm_ref)
    lat = lax.axis_index("lat")
    even = lax.rem(lat, 2) == 0
    poles = (lat == 0, lat == lax.axis_size("lat") - 1)
    cols = f2.shape[-2]
    total = out_ref.shape[1]
    span = 4 * cols
    units = [(b, side) for b in range(p_ref.shape[0]) for side in range(2)]
    for u, (b, side) in enumerate(units):
        pole = poles[side]
        moved = pole if side == 0 else jnp.logical_not(pole)
        from_p = even if side == 0 else jnp.logical_not(even)
        base = jnp.where(moved, 1, 0)
        close = jnp.where(moved, 0, HALO - 1)
        for k in range(HALO):
            taps = three_taps(jnp.where(from_p, p_ref[b, k], q_ref[b, k]))
            x3[u, base + k] = taps
        x3[u, 6 if side == 0 else 11] = x3[u, base + close]
        for k in range(HALO):
            taps = three_taps(jnp.where(from_p, p_own_ref[b, k], q_own_ref[b, k]))
            x3[u, (7 if side == 0 else 6) + k] = taps
            if k == (0 if side == 0 else HALO - 1):
                x3[u, jnp.where(moved, 0, HALO)] = taps
    for u, (b, side) in enumerate(units):
        pole = poles[side]
        v = near_block(
            [[x3[u, first + i] for i in range(4)] for first in (0, 2, 6, 8)], wn_ref
        ).astype(BF)
        for q in range(2):
            for o, piece in enumerate(halves(v, q, 128)):
                c = 2 * q + o
                spread(f2, (u, side, jnp.where(pole, 3 - c, c)), side, piece)
            for o, piece in enumerate(halves(v, 2 + q, 128)):
                spread(f2, (u, side, 2 * q + o), 1 - side, piece)
        for h in range(2):
            for c in range(4):
                spread(f2, (u, 1 - side, c), h, fx_ref[b, side, h, c])
    for u in range(len(units)):
        s[u * span : (u + 1) * span] = far_block((f2, (u, 0)), (f2, (u, 1)), wf_ref)
    copies = []
    for u, (b, side) in enumerate(units):
        done = dot(s[u * span : (u + 1) * span], wm_ref[...]).astype(BF)
        for c in range(4):
            for h in range(2):
                y[u, 4 * h + c] = done[cols * c : cols * c + cols, 128 * h : 128 * h + 128]
        to = out_ref.at[b, pl.ds(0 if side == 0 else total - 8, 8)]
        copy = pltpu.make_async_copy(y.at[u], to, sems.at[u])
        copy.start()
        copies.append(copy)
    for copy in copies:
        copy.wait()


def whole(shape):
    return pl.BlockSpec(shape, lambda *_: (0,) * len(shape))


def per_sample(shape):
    return pl.BlockSpec((1,) + shape[1:], lambda b, *_: (b,) + (0,) * (len(shape) - 1))


def params(mib):
    return pltpu.CompilerParams(vmem_limit_bytes=mib * MIB)


def cost(flops, nbytes):
    return pl.CostEstimate(flops=flops, bytes_accessed=nbytes, transcendentals=0)


def swaps(lats, lons, offset):
    half = lons // 2
    pairs = []
    for lat in range(lats):
        other = lat + (1 if (lat + offset) % 2 == 0 else -1)
        for lon in range(lons):
            if 0 <= other < lats:
                pairs.append((lon * lats + other, lon * lats + lat))
            else:
                pairs.append(((lon + half) % lons * lats + lat, lon * lats + lat))
    return pairs


def made_weights():
    return [pltpu.VMEM(shape, BF) for shape in ((4, 256, 256), (6 * 256, 256), (256, 256))]


def edge_shape(x):
    per = 128 // SLOT
    return (x.shape[0], -(-x.shape[1] // per), x.shape[2], 128)


def call_pack(x):
    edge = edge_shape(x)
    return pl.pallas_call(
        pack_columns,
        grid=(x.shape[0],),
        in_specs=[
            pl.BlockSpec(
                (1, 128 // SLOT, x.shape[2], x.shape[3]), functools.partial(lambda g, b: (b, g, 0, 0), g)
            )
            for g in range(edge[1])
        ],
        out_specs=[per_sample(edge)] * 2,
        out_shape=[jax.ShapeDtypeStruct(edge, BF)] * 2,
        compiler_params=params(PACK_MIB),
        cost_estimate=cost(0, 4 * MIB),
        name="pack_columns",
    )(*[x] * edge[1])


def call_first(x, weights):
    batch, rows, _, cols = x.shape
    chan = weights[-1].shape[1]
    first = (batch, rows // 8 - 1, 2, 4, cols, chan)
    return pl.pallas_call(
        first_rows,
        grid=(batch,),
        in_specs=[per_sample(x.shape)] + [whole(w.shape) for w in weights[:2]],
        out_specs=per_sample(first),
        out_shape=jax.ShapeDtypeStruct(first, BF),
        scratch_shapes=[pltpu.VMEM((10, cols, 256), BF)] * (rows // 8 - 1) + [made_weights()[0]],
        compiler_params=params(FIRST_MIB),
        cost_estimate=cost(6 * 10**9, 9 * MIB),
        name="first_rows",
    )(x, *weights[:2])


def call_inner(first, west, east, right, left, weights, rows):
    batch, blocks, _, _, cols, chan = first.shape
    fx = (batch, 2, 2, 4, 128, chan)
    inner = rows - 16
    return pl.pallas_call(
        inner_rows,
        grid=(batch,),
        in_specs=[per_sample(first.shape)]
        + [per_sample(right.shape)] * 4
        + [whole(w.shape) for w in weights],
        out_specs=[
            pl.BlockSpec(
                (pl.Element(1), pl.Element(inner), pl.Element(cols), pl.Element(chan)),
                lambda b: (b, 8, 0, 0),
            ),
            per_sample(fx),
        ],
        out_shape=[
            jax.ShapeDtypeStruct((batch, rows, cols, chan), BF),
            jax.ShapeDtypeStruct(fx, BF),
        ],
        scratch_shapes=[
            pltpu.VMEM((rows, 16, 256), BF),
        ]
        + [pltpu.VMEM((3, 4, cols, 256), BF)] * blocks
        + [pltpu.VMEM(((blocks - 1) * 4 * cols, 256), BF)]
        + made_weights(),
        compiler_params=params(INNER_MIB),
        cost_estimate=cost(7 * 10**9, 12 * MIB),
        name="inner_rows",
    )(first, west, east, right, left, *weights)


def on_device(fields, lift_weight, near_kernel, far_kernel, mix_weight):
    batch, rows, cols, cin = fields.shape
    chan = mix_weight.shape[1]
    lats, lons = lax.axis_size("lat"), lax.axis_size("lon")
    x = jnp.transpose(fields, (0, 1, 3, 2))
    edge = edge_shape(x)
    west, east = call_pack(x)
    right = lax.ppermute(west, "lon", [((i + 1) % lons, i) for i in range(lons)])
    left = lax.ppermute(east, "lon", [((i - 1) % lons, i) for i in range(lons)])
    weights = (lift_weight, near_kernel, far_kernel, mix_weight)
    first = call_first(x, weights)
    strip = (batch, HALO, cin, 128)
    last = rows // 8 - 1
    p_send, q_send = pl.pallas_call(
        functools.partial(pack_rows, rows),
        grid=(batch,),
        in_specs=[
            pl.BlockSpec((1, 8, cin, cols), lambda b: (b, 0, 0, 0)),
            pl.BlockSpec((1, 8, cin, cols), lambda b: (b, last, 0, 0)),
            per_sample(edge),
            per_sample(edge),
        ],
        out_specs=[per_sample(strip)] * 2,
        out_shape=[jax.ShapeDtypeStruct(strip, BF)] * 2,
        compiler_params=params(PACK_MIB),
        cost_estimate=cost(0, 2 * MIB),
        name="pack_rows",
    )(x, x, right, left)
    p_got = lax.ppermute(p_send, ("lon", "lat"), swaps(lats, lons, 1))
    q_got = lax.ppermute(q_send, ("lon", "lat"), swaps(lats, lons, 0))

    out, edges = call_inner(first, west, east, right, left, weights, rows)
    units = 2 * batch
    fx = edges.shape
    made = made_weights()
    return pl.pallas_call(
        outer_rows,
        grid=(1,),
        in_specs=[whole(strip)] * 4
        + [whole(fx)]
        + [whole(w.shape) for w in weights]
        + [pl.BlockSpec(memory_space=pl.ANY)],
        out_specs=pl.BlockSpec(memory_space=pl.ANY),
        out_shape=jax.ShapeDtypeStruct((batch, rows, cols, chan), BF),
        scratch_shapes=[
            pltpu.VMEM((units, 12, 128, 256), BF),
            pltpu.VMEM((3, units, 2, 4, cols, 256), BF),
            pltpu.VMEM((units * 4 * cols, 256), BF),
            pltpu.VMEM((units, 8, cols, chan), BF),
        ]
        + made
        + [pltpu.SemaphoreType.DMA((units,))],
        input_output_aliases={9: 0},
        compiler_params=params(OUTER_MIB),
        cost_estimate=cost(5 * 10**9, 6 * MIB),
        name="outer_rows",
    )(p_send, q_send, p_got, q_got, edges, *weights, out)


def solution(mesh):
    return jax.shard_map(
        on_device,
        mesh=mesh,
        in_specs=(P(None, "lat", "lon", None), P(), P(), P(), P()),
        out_specs=P(None, "lat", "lon", None),
        check_vma=False,
    )
```

```python
import functools

import jax
import jax.numpy as jnp
from jax import lax
from jax.experimental import pallas as pl
from jax.experimental.pallas import tpu as pltpu
from jax.sharding import PartitionSpec as P

FAR = 4
BF = jnp.bfloat16
F32 = jnp.float32
HALO = 5
SLOT = 8
WIDE = 1
EVERY = 4
MIB = 1 << 20
MADE = ((4, 256, 256), (6 * 256, 256), (256, 256))
FIRST_MIB = 16
INNER_MIB = 24
OUTER_MIB = 34
PACK_MIB = 12


def dot(a, b):
    return jnp.dot(a, b, preferred_element_type=F32)


def silu_of_half(h):
    return h + h * jnp.tanh(h)


def turned(v, shift):
    shift %= 128
    if shift == 0:
        return v
    return jnp.concatenate([v[:, 128 - shift :], v[:, : 128 - shift]], axis=1)


def widened(row):
    return jnp.concatenate([row, jnp.zeros((row.shape[0], 128 - row.shape[1]), BF)], axis=1)


def with_columns(row, right_ref, left_ref, lead, r):
    per = 128 // SLOT
    cols = row.shape[1]
    at = (r % per) * SLOT
    right = turned(right_ref[lead, r // per], cols - at)
    left = turned(left_ref[lead, r // per], 128 - SLOT - at)
    return jnp.concatenate([row, right[:, cols : cols + SLOT], left[:, cols + SLOT :]], axis=1)


def three_taps(row):
    cin = row.shape[0]
    fill = jnp.zeros((256 - 3 * cin, 128), BF)
    tall = jnp.concatenate([row, row, row, fill], axis=0).T
    lane = lax.broadcasted_iota(jnp.int32, (128, 128), 1)
    low, high = tall[:, :128], tall[:, 128:]
    before = jnp.concatenate([low[127:], low[:127]], axis=0)
    after = jnp.concatenate([high[1:], high[:1]], axis=0)
    low = jnp.where(lane < cin, before, low)
    high = jnp.where(lane < 2 * cin - 128, high, after)
    return jnp.concatenate([low, high], axis=1)


def pack_columns(*refs):
    *x_refs, west_ref, east_ref = refs
    lane = lax.broadcasted_iota(jnp.int32, (west_ref.shape[2], 128), 1)
    for group, x_ref in enumerate(x_refs):
        cols = x_ref.shape[3]
        rows = [widened(x_ref[0, i]) for i in range(x_ref.shape[1])]
        moved = [turned(row, i * SLOT) for i, row in enumerate(rows)]
        offset = cols - SLOT
        west, east = moved[0], moved[0]
        for i, row in enumerate(moved):
            west = jnp.where(lane < i * SLOT, west, row)
            at = (i * SLOT + offset) % 128
            east = jnp.where((lane >= at) & (lane < at + SLOT), row, east)
        west_ref[0, group] = west
        east_ref[0, group] = turned(east, -offset)


def make_near(lift_ref, near_ref, wn_ref):
    cin, chan = lift_ref.shape
    wn_ref[...] = jnp.zeros_like(wn_ref)
    for a in range(3):
        for b in range(3):
            near = (0.5 * dot(lift_ref[...], near_ref[a, b])).astype(BF)
            for o in range(2):
                wn_ref[a + o, b * cin : (b + 1) * cin, o * chan : (o + 1) * chan] = near


def make_far(far_ref, mix_ref, wf_ref, wm_ref):
    chan = mix_ref.shape[0]
    wf_ref[...] = jnp.zeros_like(wf_ref)
    wm_ref[...] = jnp.zeros_like(wm_ref)
    for a in range(3):
        for b in range(3):
            far = (0.5 * far_ref[a, b].astype(F32)).astype(BF)
            for o in range(2):
                k = a + o
                base = (2 * b + k // 2) * 256 + (k % 2) * chan
                wf_ref[base : base + chan, o * chan : (o + 1) * chan] = far
    wm_ref[:chan, :chan] = mix_ref[...]
    wm_ref[chan:, chan:] = mix_ref[...]


def pack_rows(rows, top_ref, bottom_ref, right_ref, left_ref, p_ref, q_ref):
    even = lax.rem(lax.axis_index("lat"), 2) == 0
    top, bottom = [], []
    for k in range(HALO):
        top.append(with_columns(top_ref[0, k], right_ref, left_ref, 0, k))
        r = rows - HALO + k
        bottom.append(with_columns(bottom_ref[0, 8 - HALO + k], right_ref, left_ref, 0, r))
    for k in range(HALO):
        p_ref[0, k] = jnp.where(even, top[k], bottom[k])
        q_ref[0, k] = jnp.where(even, bottom[k], top[k])


def spread(f2, at, half, piece):
    turned_piece = jnp.concatenate([piece[128 - FAR :], piece[: 128 - FAR]], axis=0)
    f2[(*at, slice(None), slice(half * 128, half * 128 + 128))] = turned_piece


def tap(ref, b, at, c):
    cols = ref.shape[-2] - 16
    return ref[(*at, c, slice(b * FAR, b * FAR + cols))]


def near_block(rows, wn_ref):
    lhs = jnp.concatenate(
        [jnp.concatenate([pair[i] for pair in rows], axis=0) for i in range(4)], axis=1
    )
    return silu_of_half(dot(lhs, wn_ref[...].reshape(4 * 256, 256)))


def far_block(uppers, lowers, wf_ref):
    lhs = jnp.concatenate(
        [
            jnp.concatenate([tap(ref, b, at, c) for ref, at in refs for c in range(4)], axis=0)
            for b in range(3)
            for refs in (uppers, lowers)
        ],
        axis=1,
    )
    return silu_of_half(dot(lhs, wf_ref[...])).astype(BF)


def halves(v, pair, height):
    base = height * pair
    return [v[base : base + height, 128 * o : 128 * o + 128] for o in range(2)]


def first_rows(x_ref, lift_ref, near_ref, first_ref, wn_ref, *x3s):

    @pl.when(pl.program_id(0) == 0)
    def _():
        make_near(lift_ref, near_ref, wn_ref)

    cols = x_ref.shape[3]
    blocks = first_ref.shape[1]

    def build(m):
        for i in range(2 if m else 0, 10):
            taps = three_taps(widened(x_ref[0, 8 * m + i + FAR - 1]))[:cols]
            x3s[m][i] = taps
            if i >= 8 and m + 1 < blocks:
                x3s[m + 1][i - 8] = taps

    def store(m, v):
        for p in range(4):
            for o, piece in enumerate(halves(v, p, cols)):
                h, c = divmod(2 * p + o, 4)
                first_ref[0, m, h, c] = piece

    build(0)
    for m in range(blocks):
        rows = [[x3s[m][2 * p + i] for i in range(4)] for p in range(4)]
        if m + 1 < blocks:
            build(m + 1)
        store(m, near_block(rows, wn_ref).astype(BF))


def joined(main, strip):
    end = main.shape[0]
    head = jnp.concatenate([strip[14:15], main[:16].astype(F32)[1:]], axis=0)
    tail = jnp.concatenate([main[end - 16 :].astype(F32)[:15], strip[1:2]], axis=0)
    beyond = jnp.concatenate([strip[2:6], strip[2:10], strip[10:14]], axis=0)
    return jnp.concatenate(
        [head.astype(BF), main[16 : end - 16], tail.astype(BF), beyond.astype(BF)], axis=0
    )


def edge_strips(b, west_ref, east_ref, right_ref, left_ref, wn_ref, strips, pairs):
    cin = west_ref.shape[2]
    per = 128 // SLOT
    lane = lax.rem(lax.broadcasted_iota(jnp.int32, (cin, 128), 1), SLOT)
    for g in range(west_ref.shape[1]):
        right = jnp.where(lane < 2, turned(east_ref[b, g], -6), turned(right_ref[b, g], 2))
        left = jnp.where(lane < 6, turned(left_ref[b, g], -2), turned(west_ref[b, g], 6))
        right, left = three_taps(right), three_taps(left)
        for i in range(per):
            at = slice(SLOT * i, SLOT * i + SLOT)
            strips[b, per * g + i] = jnp.concatenate([right[at], left[at]], axis=0)
    low = FAR - 1
    rows = [[strips[b, low + 2 * q + i] for i in range(4)] for q in range(pairs)]
    return near_block(rows, wn_ref)


def inner_rows(
    first_ref, west_ref, east_ref, right_ref, left_ref, wn_ref, far_ref, mix_ref,
    out_ref, fx_ref, wf_ref, wm_ref, strips, edge, s, *f2s,
):
    blocks = len(f2s)
    cols = f2s[0].shape[-2] - 16
    pairs = 4 * blocks

    @pl.when(pl.program_id(0) == 0)
    def _():
        make_far(far_ref, mix_ref, wf_ref, wm_ref)
        for b in range(west_ref.shape[0]):
            edge[b] = edge_strips(
                b, west_ref, east_ref, right_ref, left_ref, wn_ref, strips, pairs
            )

    sample = pl.program_id(0)
    span = 4 * cols

    def far(g):
        near, next_ = ([(f2s[i + k], ()) for i in range(g, g + WIDE)] for k in range(2))
        s[g * span : (g + WIDE) * span] = far_block(near, next_, wf_ref)

    for m in range(blocks):
        for p in range(4):
            q = 4 * m + p
            for o, strip in enumerate(halves(edge[sample, 16 * q : 16 * q + 16], 0, 16)):
                h, c = divmod(2 * p + o, 4)
                piece = joined(first_ref[0, m, h, c], strip)
                spread(f2s[m], (c,), h, piece)
                if m == 0:
                    fx_ref[0, 0, h, c] = piece
                if m == blocks - 1:
                    fx_ref[0, 1, h, c] = piece
        if m >= WIDE and (m - WIDE) % WIDE == 0:
            far(m - WIDE)
    y = dot(s[...], wm_ref[...]).astype(BF)
    for g in range(blocks - 1):
        for c in range(4):
            at = g * span + c * cols
            for h in range(2):
                out_ref[0, 8 * g + 4 * h + c] = y[at : at + cols, 128 * h : 128 * h + 128]


def outer_rows(
    p_own_ref, q_own_ref, p_ref, q_ref, fx_ref,
    wn_ref, wf_ref, wm_ref, _, out_ref, x3, f2, s, y, sems,
):
    lat = lax.axis_index("lat")
    even = lax.rem(lat, 2) == 0
    poles = (lat == 0, lat == lax.axis_size("lat") - 1)
    cols = f2.shape[-2] - 16
    total = out_ref.shape[1]
    span = 4 * cols
    units = [(b, side) for b in range(p_ref.shape[0]) for side in range(2)]
    for u, (b, side) in enumerate(units):
        pole = poles[side]
        moved = pole if side == 0 else jnp.logical_not(pole)
        from_p = even if side == 0 else jnp.logical_not(even)
        base = jnp.where(moved, 1, 0)
        close = jnp.where(moved, 0, HALO - 1)
        for k in range(HALO):
            taps = three_taps(jnp.where(from_p, p_ref[b, k], q_ref[b, k]))
            x3[u, base + k] = taps
        x3[u, 6 if side == 0 else 11] = x3[u, base + close]
        for k in range(HALO):
            taps = three_taps(jnp.where(from_p, p_own_ref[b, k], q_own_ref[b, k]))
            x3[u, (7 if side == 0 else 6) + k] = taps
            if k == (0 if side == 0 else HALO - 1):
                x3[u, jnp.where(moved, 0, HALO)] = taps
    for u, (b, side) in enumerate(units):
        pole = poles[side]
        v = near_block(
            [[x3[u, first + i] for i in range(4)] for first in (0, 2, 6, 8)], wn_ref
        ).astype(BF)
        for q in range(2):
            for o, piece in enumerate(halves(v, q, 128)):
                c = 2 * q + o
                spread(f2, (u, side, jnp.where(pole, 3 - c, c)), side, piece)
            for o, piece in enumerate(halves(v, 2 + q, 128)):
                spread(f2, (u, side, 2 * q + o), 1 - side, piece)
        for h in range(2):
            for c in range(4):
                spread(f2, (u, 1 - side, c), h, fx_ref[b, side, h, c])
    copies = []

    def finish(u):
        b, side = units[u]
        done = dot(s[u * span : (u + 1) * span], wm_ref[...]).astype(BF)
        for c in range(4):
            for h in range(2):
                y[u, 4 * h + c] = done[cols * c : cols * c + cols, 128 * h : 128 * h + 128]
        to = out_ref.at[b, pl.ds(0 if side == 0 else total - 8, 8)]
        copy = pltpu.make_async_copy(y.at[u], to, sems.at[u])
        copy.start()
        copies.append(copy)

    for u in range(len(units)):
        s[u * span : (u + 1) * span] = far_block([(f2, (u, 0))], [(f2, (u, 1))], wf_ref)
        if (u + 1) % EVERY == 0:
            for done_unit in range(u + 1 - EVERY, u + 1):
                finish(done_unit)
    for copy in copies:
        copy.wait()


def whole(shape):
    return pl.BlockSpec(shape, lambda *_: (0,) * len(shape))


def per_sample(shape):
    return pl.BlockSpec((1,) + shape[1:], lambda b, *_: (b,) + (0,) * (len(shape) - 1))


def params(mib):
    return pltpu.CompilerParams(vmem_limit_bytes=mib * MIB)


def cost(flops, nbytes):
    return pl.CostEstimate(flops=flops, bytes_accessed=nbytes, transcendentals=0)


def swaps(lats, lons, offset):
    half = lons // 2
    pairs = []
    for lat in range(lats):
        other = lat + (1 if (lat + offset) % 2 == 0 else -1)
        for lon in range(lons):
            if 0 <= other < lats:
                pairs.append((lon * lats + other, lon * lats + lat))
            else:
                pairs.append(((lon + half) % lons * lats + lat, lon * lats + lat))
    return pairs


def edge_shape(x):
    per = 128 // SLOT
    return (x.shape[0], -(-x.shape[1] // per), x.shape[2], 128)


def call_pack(x):
    edge = edge_shape(x)
    return pl.pallas_call(
        pack_columns,
        grid=(x.shape[0],),
        in_specs=[
            pl.BlockSpec(
                (1, 128 // SLOT, x.shape[2], x.shape[3]), functools.partial(lambda g, b: (b, g, 0, 0), g)
            )
            for g in range(edge[1])
        ],
        out_specs=[per_sample(edge)] * 2,
        out_shape=[jax.ShapeDtypeStruct(edge, BF)] * 2,
        compiler_params=params(PACK_MIB),
        cost_estimate=cost(0, 4 * MIB),
        name="pack_columns",
    )(*[x] * edge[1])


def call_first(x, weights):
    batch, rows, _, cols = x.shape
    chan = weights[-1].shape[1]
    first = (batch, rows // 8 - 1, 2, 4, cols, chan)
    return pl.pallas_call(
        first_rows,
        grid=(batch,),
        in_specs=[per_sample(x.shape)] + [whole(w.shape) for w in weights[:2]],
        out_specs=[per_sample(first), whole(MADE[0])],
        out_shape=[jax.ShapeDtypeStruct(shape, BF) for shape in (first, MADE[0])],
        scratch_shapes=[pltpu.VMEM((10, cols, 256), BF)] * (rows // 8 - 1),
        compiler_params=params(FIRST_MIB),
        cost_estimate=cost(6 * 10**9, 9 * MIB),
        name="first_rows",
    )(x, *weights[:2])


def call_inner(first, wn, west, east, right, left, weights, rows):
    batch, blocks, _, _, cols, chan = first.shape
    fx = (batch, 2, 2, 4, 128, chan)
    inner = rows - 16
    return pl.pallas_call(
        inner_rows,
        grid=(batch,),
        in_specs=[per_sample(first.shape)]
        + [whole(right.shape)] * 4
        + [whole(w.shape) for w in (wn, *weights[2:])],
        out_specs=[
            pl.BlockSpec(
                (pl.Element(1), pl.Element(inner), pl.Element(cols), pl.Element(chan)),
                lambda b: (b, 8, 0, 0),
            ),
            per_sample(fx),
            whole(MADE[1]),
            whole(MADE[2]),
        ],
        out_shape=[
            jax.ShapeDtypeStruct(shape, BF)
            for shape in ((batch, rows, cols, chan), fx, MADE[1], MADE[2])
        ],
        scratch_shapes=[
            pltpu.VMEM((batch, rows, 16, 256), BF),
            pltpu.VMEM((batch, 16 * 4 * blocks, 256), F32),
            pltpu.VMEM(((blocks - 1) * 4 * cols, 256), BF),
        ]
        + [pltpu.VMEM((4, cols + 16, 256), BF)] * blocks,
        compiler_params=params(INNER_MIB),
        cost_estimate=cost(7 * 10**9, 12 * MIB),
        name="inner_rows",
    )(first, west, east, right, left, wn, *weights[2:])


def on_device(fields, lift_weight, near_kernel, far_kernel, mix_weight):
    batch, rows, cols, cin = fields.shape
    chan = mix_weight.shape[1]
    lats, lons = lax.axis_size("lat"), lax.axis_size("lon")
    x = jnp.transpose(fields, (0, 1, 3, 2))
    edge = edge_shape(x)
    west, east = call_pack(x)
    right = lax.ppermute(west, "lon", [((i + 1) % lons, i) for i in range(lons)])
    left = lax.ppermute(east, "lon", [((i - 1) % lons, i) for i in range(lons)])
    weights = (lift_weight, near_kernel, far_kernel, mix_weight)
    first, wn = call_first(x, weights)
    strip = (batch, HALO, cin, 128)
    last = rows // 8 - 1
    p_send, q_send = pl.pallas_call(
        functools.partial(pack_rows, rows),
        grid=(batch,),
        in_specs=[
            pl.BlockSpec((1, 8, cin, cols), lambda b: (b, 0, 0, 0)),
            pl.BlockSpec((1, 8, cin, cols), lambda b: (b, last, 0, 0)),
            per_sample(edge),
            per_sample(edge),
        ],
        out_specs=[per_sample(strip)] * 2,
        out_shape=[jax.ShapeDtypeStruct(strip, BF)] * 2,
        compiler_params=params(PACK_MIB),
        cost_estimate=cost(0, 2 * MIB),
        name="pack_rows",
    )(x, x, right, left)
    p_got = lax.ppermute(p_send, ("lon", "lat"), swaps(lats, lons, 1))
    q_got = lax.ppermute(q_send, ("lon", "lat"), swaps(lats, lons, 0))

    out, edges, wf, wm = call_inner(first, wn, west, east, right, left, weights, rows)
    units = 2 * batch
    fx = edges.shape
    return pl.pallas_call(
        outer_rows,
        grid=(1,),
        in_specs=[whole(strip)] * 4
        + [whole(fx)]
        + [whole(shape) for shape in MADE]
        + [pl.BlockSpec(memory_space=pl.ANY)],
        out_specs=pl.BlockSpec(memory_space=pl.ANY),
        out_shape=jax.ShapeDtypeStruct((batch, rows, cols, chan), BF),
        scratch_shapes=[
            pltpu.VMEM((units, 12, 128, 256), BF),
            pltpu.VMEM((units, 2, 4, cols + 16, 256), BF),
            pltpu.VMEM((units * 4 * cols, 256), BF),
            pltpu.VMEM((units, 8, cols, chan), BF),
            pltpu.SemaphoreType.DMA((units,)),
        ],
        input_output_aliases={8: 0},
        compiler_params=params(OUTER_MIB),
        cost_estimate=cost(5 * 10**9, 6 * MIB),
        name="outer_rows",
    )(p_send, q_send, p_got, q_got, edges, wn, wf, wm, out)


def solution(mesh):
    return jax.shard_map(
        on_device,
        mesh=mesh,
        in_specs=(P(None, "lat", "lon", None), P(), P(), P(), P()),
        out_specs=P(None, "lat", "lon", None),
        check_vma=False,
    )
```

```python
import functools

import jax
import jax.numpy as jnp
from jax import lax
from jax.experimental import pallas as pl
from jax.experimental.pallas import tpu as pltpu
from jax.sharding import PartitionSpec as P

FAR = 4
BF = jnp.bfloat16
F32 = jnp.float32
HALO = 5
SLOT = 8
WIDE = 1
EVERY = 2
MIB = 1 << 20
MADE = ((4, 256, 256), (6 * 256, 256), (256, 256))
FIRST_MIB = 16
INNER_MIB = 20
OUTER_MIB = 30
PACK_MIB = 12


def dot(a, b):
    return jnp.dot(a, b, preferred_element_type=F32)


def silu_of_half(h):
    return h + h * jnp.tanh(h)


def turned(v, shift):
    shift %= 128
    if shift == 0:
        return v
    return jnp.concatenate([v[:, 128 - shift :], v[:, : 128 - shift]], axis=1)


def widened(row):
    return jnp.concatenate([row, jnp.zeros((row.shape[0], 128 - row.shape[1]), BF)], axis=1)


def with_columns(row, right_ref, left_ref, lead, r):
    per = 128 // SLOT
    cols = row.shape[1]
    at = (r % per) * SLOT
    right = turned(right_ref[lead, r // per], cols - at)
    left = turned(left_ref[lead, r // per], 128 - SLOT - at)
    return jnp.concatenate([row, right[:, cols : cols + SLOT], left[:, cols + SLOT :]], axis=1)


def three_taps(row):
    cin = row.shape[0]
    fill = jnp.zeros((256 - 3 * cin, 128), BF)
    tall = jnp.concatenate([row, row, row, fill], axis=0).T
    lane = lax.broadcasted_iota(jnp.int32, (128, 128), 1)
    low, high = tall[:, :128], tall[:, 128:]
    before = jnp.concatenate([low[127:], low[:127]], axis=0)
    after = jnp.concatenate([high[1:], high[:1]], axis=0)
    low = jnp.where(lane < cin, before, low)
    high = jnp.where(lane < 2 * cin - 128, high, after)
    return jnp.concatenate([low, high], axis=1)


def pack_columns(*refs):
    *x_refs, west_ref, east_ref, choice = refs
    per = 128 // SLOT
    offset = x_refs[0].shape[3] - SLOT

    @pl.when(pl.program_id(0) == 0)
    def _():
        source = lax.broadcasted_iota(jnp.int32, (128, 256), 0)
        target = lax.broadcasted_iota(jnp.int32, (128, 256), 1)
        is_east = target >= 128
        lane = jnp.where(is_east, target - 128, target)
        wanted = jnp.where(is_east, offset, 0) + lax.rem(lane, SLOT)
        same = source == wanted
        spot = lane // SLOT
        for i in range(per):
            keep = jnp.where(same & (spot == i), 1.0, 0.0)
            choice[i * 128 : i * 128 + 128] = keep.astype(BF)

    lhs = jnp.concatenate(
        [
            jnp.concatenate([widened(x_ref[0, i]) for i in range(per)], axis=1)
            for x_ref in x_refs
        ],
        axis=0,
    )
    packed = dot(lhs, choice[...]).astype(BF)
    cin = x_refs[0].shape[2]
    for group in range(len(x_refs)):
        rows = slice(group * cin, group * cin + cin)
        west_ref[0, group] = packed[rows, :128]
        east_ref[0, group] = packed[rows, 128:]


def make_near(lift_ref, near_ref, wn_ref):
    cin, chan = lift_ref.shape
    wn_ref[...] = jnp.zeros_like(wn_ref)
    for a in range(3):
        for b in range(3):
            near = (0.5 * dot(lift_ref[...], near_ref[a, b])).astype(BF)
            for o in range(2):
                wn_ref[a + o, b * cin : (b + 1) * cin, o * chan : (o + 1) * chan] = near


def make_far(far_ref, mix_ref, wf_ref, wm_ref):
    chan = mix_ref.shape[0]
    wf_ref[...] = jnp.zeros_like(wf_ref)
    wm_ref[...] = jnp.zeros_like(wm_ref)
    for a in range(3):
        for b in range(3):
            far = (0.5 * far_ref[a, b].astype(F32)).astype(BF)
            for o in range(2):
                k = a + o
                base = (2 * b + k // 2) * 256 + (k % 2) * chan
                wf_ref[base : base + chan, o * chan : (o + 1) * chan] = far
    wm_ref[:chan, :chan] = mix_ref[...]
    wm_ref[chan:, chan:] = mix_ref[...]


def pack_rows(rows, top_ref, bottom_ref, right_ref, left_ref, p_ref, q_ref):
    even = lax.rem(lax.axis_index("lat"), 2) == 0
    top, bottom = [], []
    for k in range(HALO):
        top.append(with_columns(top_ref[0, k], right_ref, left_ref, 0, k))
        r = rows - HALO + k
        bottom.append(with_columns(bottom_ref[0, 8 - HALO + k], right_ref, left_ref, 0, r))
    for k in range(HALO):
        p_ref[0, k] = jnp.where(even, top[k], bottom[k])
        q_ref[0, k] = jnp.where(even, bottom[k], top[k])


def spread(f2, at, half, piece):
    turned_piece = jnp.concatenate([piece[128 - FAR :], piece[: 128 - FAR]], axis=0)
    f2[(*at, slice(None), slice(half * 128, half * 128 + 128))] = turned_piece


def tap(ref, b, at, c):
    cols = ref.shape[-2] - 16
    return ref[(*at, c, slice(b * FAR, b * FAR + cols))]


def near_block(rows, wn_ref):
    lhs = jnp.concatenate(
        [jnp.concatenate([pair[i] for pair in rows], axis=0) for i in range(4)], axis=1
    )
    return silu_of_half(dot(lhs, wn_ref[...].reshape(4 * 256, 256)))


def far_block(uppers, lowers, wf_ref):
    lhs = jnp.concatenate(
        [
            jnp.concatenate([tap(ref, b, at, c) for ref, at in refs for c in range(4)], axis=0)
            for b in range(3)
            for refs in (uppers, lowers)
        ],
        axis=1,
    )
    return silu_of_half(dot(lhs, wf_ref[...])).astype(BF)


def halves(v, pair, height):
    base = height * pair
    return [v[base : base + height, 128 * o : 128 * o + 128] for o in range(2)]


def first_rows(
    x_ref, lift_ref, near_ref, far_ref, mix_ref, first_ref, wn_ref, wf_ref, wm_ref, *x3s
):

    @pl.when(pl.program_id(0) == 0)
    def _():
        make_near(lift_ref, near_ref, wn_ref)
        make_far(far_ref, mix_ref, wf_ref, wm_ref)

    cols = x_ref.shape[3]
    blocks = first_ref.shape[1]

    def build(m):
        for i in range(2 if m else 0, 10):
            taps = three_taps(widened(x_ref[0, 8 * m + i + FAR - 1]))[:cols]
            x3s[m][i] = taps
            if i >= 8 and m + 1 < blocks:
                x3s[m + 1][i - 8] = taps

    def store(m, v):
        for p in range(4):
            for o, piece in enumerate(halves(v, p, cols)):
                h, c = divmod(2 * p + o, 4)
                first_ref[0, m, h, c] = piece

    build(0)
    for m in range(blocks):
        rows = [[x3s[m][2 * p + i] for i in range(4)] for p in range(4)]
        if m + 1 < blocks:
            build(m + 1)
        store(m, near_block(rows, wn_ref).astype(BF))


def joined(main, strip):
    end = main.shape[0]
    head = jnp.concatenate([strip[14:15], main[:16].astype(F32)[1:]], axis=0)
    tail = jnp.concatenate([main[end - 16 :].astype(F32)[:15], strip[1:2]], axis=0)
    beyond = jnp.concatenate([strip[2:6], strip[2:10], strip[10:14]], axis=0)
    return jnp.concatenate(
        [head.astype(BF), main[16 : end - 16], tail.astype(BF), beyond.astype(BF)], axis=0
    )


def build_strips(b, west_ref, east_ref, right_ref, left_ref, strips):
    cin = west_ref.shape[2]
    per = 128 // SLOT
    lane = lax.rem(lax.broadcasted_iota(jnp.int32, (cin, 128), 1), SLOT)
    for g in range(west_ref.shape[1]):
        right = jnp.where(lane < 2, turned(east_ref[b, g], -6), turned(right_ref[b, g], 2))
        left = jnp.where(lane < 6, turned(left_ref[b, g], -2), turned(west_ref[b, g], 6))
        right, left = three_taps(right), three_taps(left)
        for i in range(per):
            at = slice(SLOT * i, SLOT * i + SLOT)
            strips[per * g + i] = jnp.concatenate([right[at], left[at]], axis=0)


def inner_rows(
    first_ref, west_ref, east_ref, right_ref, left_ref, wn_ref, wf_ref, wm_ref,
    out_ref, fx_ref, edge, s, *scratch,
):
    batch = west_ref.shape[0]
    strips, f2s = scratch[:batch], scratch[batch:]
    blocks = len(f2s)
    cols = f2s[0].shape[-2] - 16
    pairs = 4 * blocks

    @pl.when(pl.program_id(0) == 0)
    def _():
        for b in range(batch + 1):
            if b < batch:
                build_strips(b, west_ref, east_ref, right_ref, left_ref, strips[b])
            if b > 0:
                rows = [
                    [strips[b - 1][FAR - 1 + 2 * q + i] for i in range(4)] for q in range(pairs)
                ]
                edge[b - 1] = near_block(rows, wn_ref)

    sample = pl.program_id(0)
    span = 4 * cols

    def far(g):
        near, next_ = ([(f2s[i + k], ()) for i in range(g, g + WIDE)] for k in range(2))
        s[g * span : (g + WIDE) * span] = far_block(near, next_, wf_ref)

    for m in range(blocks):
        for p in range(4):
            q = 4 * m + p
            for o, strip in enumerate(halves(edge[sample, 16 * q : 16 * q + 16], 0, 16)):
                h, c = divmod(2 * p + o, 4)
                piece = joined(first_ref[0, m, h, c], strip)
                spread(f2s[m], (c,), h, piece)
                if m == 0:
                    fx_ref[0, 0, h, c] = piece
                if m == blocks - 1:
                    fx_ref[0, 1, h, c] = piece
        if m >= WIDE and (m - WIDE) % WIDE == 0:
            far(m - WIDE)
    y = dot(s[...], wm_ref[...]).astype(BF)
    for g in range(blocks - 1):
        for c in range(4):
            at = g * span + c * cols
            for h in range(2):
                out_ref[0, 8 * g + 4 * h + c] = y[at : at + cols, 128 * h : 128 * h + 128]


def outer_rows(
    p_own_ref, q_own_ref, p_ref, q_ref, fx_ref,
    wn_ref, wf_ref, wm_ref, _, out_ref, s, y, sems, *scratch,
):
    lat = lax.axis_index("lat")
    even = lax.rem(lat, 2) == 0
    poles = (lat == 0, lat == lax.axis_size("lat") - 1)
    units = [(b, side) for b in range(p_ref.shape[0]) for side in range(2)]
    count = len(units)
    x3s, f2s = scratch[:count], scratch[count:]
    cols = f2s[0].shape[-2] - 16
    total = out_ref.shape[1]
    span = 4 * cols

    def build(u):
        b, side = units[u]
        x3 = x3s[u]
        pole = poles[side]
        moved = pole if side == 0 else jnp.logical_not(pole)
        from_p = even if side == 0 else jnp.logical_not(even)
        base = jnp.where(moved, 1, 0)
        close = jnp.where(moved, 0, HALO - 1)
        for k in range(HALO):
            x3[base + k] = three_taps(jnp.where(from_p, p_ref[b, k], q_ref[b, k]))
        x3[6 if side == 0 else 11] = x3[base + close]
        for k in range(HALO):
            taps = three_taps(jnp.where(from_p, p_own_ref[b, k], q_own_ref[b, k]))
            x3[(7 if side == 0 else 6) + k] = taps
            if k == (0 if side == 0 else HALO - 1):
                x3[jnp.where(moved, 0, HALO)] = taps

    def first(u):
        b, side = units[u]
        pole = poles[side]
        rows = [[x3s[u][at + i] for i in range(4)] for at in (0, 2, 6, 8)]
        v = near_block(rows, wn_ref).astype(BF)
        for q in range(2):
            for o, piece in enumerate(halves(v, q, 128)):
                c = 2 * q + o
                spread(f2s[u], (side, jnp.where(pole, 3 - c, c)), side, piece)
            for o, piece in enumerate(halves(v, 2 + q, 128)):
                spread(f2s[u], (side, 2 * q + o), 1 - side, piece)

    def known(u):
        b, side = units[u]
        for h in range(2):
            for c in range(4):
                spread(f2s[u], (1 - side, c), h, fx_ref[b, side, h, c])

    copies = []

    def finish(u):
        b, side = units[u]
        done = dot(s[u * span : (u + 1) * span], wm_ref[...]).astype(BF)
        for c in range(4):
            for h in range(2):
                y[u, 4 * h + c] = done[cols * c : cols * c + cols, 128 * h : 128 * h + 128]
        to = out_ref.at[b, pl.ds(0 if side == 0 else total - 8, 8)]
        copy = pltpu.make_async_copy(y.at[u], to, sems.at[u])
        copy.start()
        copies.append(copy)

    build(0)
    for u in range(count):
        if u + 1 < count:
            build(u + 1)
        known(u)
        first(u)
    for u in range(count):
        s[u * span : (u + 1) * span] = far_block([(f2s[u], (0,))], [(f2s[u], (1,))], wf_ref)
        if (u + 1) % EVERY == 0:
            for done_unit in range(u + 1 - EVERY, u + 1):
                finish(done_unit)
    for copy in copies:
        copy.wait()


def whole(shape):
    return pl.BlockSpec(shape, lambda *_: (0,) * len(shape))


def per_sample(shape):
    return pl.BlockSpec((1,) + shape[1:], lambda b, *_: (b,) + (0,) * (len(shape) - 1))


def params(mib):
    return pltpu.CompilerParams(vmem_limit_bytes=mib * MIB)


def cost(flops, nbytes):
    return pl.CostEstimate(flops=flops, bytes_accessed=nbytes, transcendentals=0)


def swaps(lats, lons, offset):
    half = lons // 2
    pairs = []
    for lat in range(lats):
        other = lat + (1 if (lat + offset) % 2 == 0 else -1)
        for lon in range(lons):
            if 0 <= other < lats:
                pairs.append((lon * lats + other, lon * lats + lat))
            else:
                pairs.append(((lon + half) % lons * lats + lat, lon * lats + lat))
    return pairs


def edge_shape(x):
    per = 128 // SLOT
    return (x.shape[0], -(-x.shape[1] // per), x.shape[2], 128)


def call_pack(x):
    edge = edge_shape(x)
    return pl.pallas_call(
        pack_columns,
        grid=(x.shape[0],),
        in_specs=[
            pl.BlockSpec(
                (1, 128 // SLOT, x.shape[2], x.shape[3]), functools.partial(lambda g, b: (b, g, 0, 0), g)
            )
            for g in range(edge[1])
        ],
        out_specs=[per_sample(edge)] * 2,
        out_shape=[jax.ShapeDtypeStruct(edge, BF)] * 2,
        scratch_shapes=[pltpu.VMEM((128 * 128 // SLOT, 256), BF)],
        compiler_params=params(PACK_MIB),
        cost_estimate=cost(0, 4 * MIB),
        name="pack_columns",
    )(*[x] * edge[1])


def call_first(x, weights):
    batch, rows, _, cols = x.shape
    chan = weights[-1].shape[1]
    first = (batch, rows // 8 - 1, 2, 4, cols, chan)
    return pl.pallas_call(
        first_rows,
        grid=(batch,),
        in_specs=[per_sample(x.shape)] + [whole(w.shape) for w in weights],
        out_specs=[per_sample(first)] + [whole(shape) for shape in MADE],
        out_shape=[jax.ShapeDtypeStruct(shape, BF) for shape in (first, *MADE)],
        scratch_shapes=[pltpu.VMEM((10, cols, 256), BF)] * (rows // 8 - 1),
        compiler_params=params(FIRST_MIB),
        cost_estimate=cost(6 * 10**9, 9 * MIB),
        name="first_rows",
    )(x, *weights)


def call_inner(first, west, east, right, left, made, rows):
    batch, blocks, _, _, cols, chan = first.shape
    fx = (batch, 2, 2, 4, 128, chan)
    inner = rows - 16
    return pl.pallas_call(
        inner_rows,
        grid=(batch,),
        in_specs=[per_sample(first.shape)]
        + [whole(right.shape)] * 4
        + [whole(shape) for shape in MADE],
        out_specs=[
            pl.BlockSpec(
                (pl.Element(1), pl.Element(inner), pl.Element(cols), pl.Element(chan)),
                lambda b: (b, 8, 0, 0),
            ),
            per_sample(fx),
        ],
        out_shape=[
            jax.ShapeDtypeStruct(shape, BF)
            for shape in ((batch, rows, cols, chan), fx)
        ],
        scratch_shapes=[
            pltpu.VMEM((batch, 16 * 4 * blocks, 256), F32),
            pltpu.VMEM(((blocks - 1) * 4 * cols, 256), BF),
        ]
        + [pltpu.VMEM((rows, 16, 256), BF)] * batch
        + [pltpu.VMEM((4, cols + 16, 256), BF)] * blocks,
        compiler_params=params(INNER_MIB),
        cost_estimate=cost(7 * 10**9, 12 * MIB),
        name="inner_rows",
    )(first, west, east, right, left, *made)


def on_device(fields, lift_weight, near_kernel, far_kernel, mix_weight):
    batch, rows, cols, cin = fields.shape
    chan = mix_weight.shape[1]
    lats, lons = lax.axis_size("lat"), lax.axis_size("lon")
    x = jnp.transpose(fields, (0, 1, 3, 2))
    edge = edge_shape(x)
    west, east = call_pack(x)
    right = lax.ppermute(west, "lon", [((i + 1) % lons, i) for i in range(lons)])
    left = lax.ppermute(east, "lon", [((i - 1) % lons, i) for i in range(lons)])
    weights = (lift_weight, near_kernel, far_kernel, mix_weight)
    first, *made = call_first(x, weights)
    strip = (batch, HALO, cin, 128)
    last = rows // 8 - 1
    p_send, q_send = pl.pallas_call(
        functools.partial(pack_rows, rows),
        grid=(batch,),
        in_specs=[
            pl.BlockSpec((1, 8, cin, cols), lambda b: (b, 0, 0, 0)),
            pl.BlockSpec((1, 8, cin, cols), lambda b: (b, last, 0, 0)),
            per_sample(edge),
            per_sample(edge),
        ],
        out_specs=[per_sample(strip)] * 2,
        out_shape=[jax.ShapeDtypeStruct(strip, BF)] * 2,
        compiler_params=params(PACK_MIB),
        cost_estimate=cost(0, 2 * MIB),
        name="pack_rows",
    )(x, x, right, left)
    p_got = lax.ppermute(p_send, ("lon", "lat"), swaps(lats, lons, 1))
    q_got = lax.ppermute(q_send, ("lon", "lat"), swaps(lats, lons, 0))

    out, edges = call_inner(first, west, east, right, left, made, rows)
    units = 2 * batch
    fx = edges.shape
    return pl.pallas_call(
        outer_rows,
        grid=(1,),
        in_specs=[whole(strip)] * 4
        + [whole(fx)]
        + [whole(shape) for shape in MADE]
        + [pl.BlockSpec(memory_space=pl.ANY)],
        out_specs=pl.BlockSpec(memory_space=pl.ANY),
        out_shape=jax.ShapeDtypeStruct((batch, rows, cols, chan), BF),
        scratch_shapes=[
            pltpu.VMEM((units * 4 * cols, 256), BF),
            pltpu.VMEM((units, 8, cols, chan), BF),
            pltpu.SemaphoreType.DMA((units,)),
        ]
        + [pltpu.VMEM((12, 128, 256), BF)] * units
        + [pltpu.VMEM((2, 4, cols + 16, 256), BF)] * units,
        input_output_aliases={8: 0},
        compiler_params=params(OUTER_MIB),
        cost_estimate=cost(5 * 10**9, 6 * MIB),
        name="outer_rows",
    )(p_send, q_send, p_got, q_got, edges, *made, out)


def solution(mesh):
    return jax.shard_map(
        on_device,
        mesh=mesh,
        in_specs=(P(None, "lat", "lon", None), P(), P(), P(), P()),
        out_specs=P(None, "lat", "lon", None),
        check_vma=False,
    )
```

```python
import functools

import jax
import jax.numpy as jnp
from jax import lax
from jax.experimental import pallas as pl
from jax.experimental.pallas import tpu as pltpu
from jax.sharding import PartitionSpec as P

FAR = 4
BF = jnp.bfloat16
F32 = jnp.float32
HALO = 5
SLOT = 8
WIDE = 1
EVERY = 2
MIB = 1 << 20
MADE = ((4, 256, 256), (6 * 256, 256), (256, 256))
FIRST_MIB = 16
INNER_MIB = 20
OUTER_MIB = 30
PACK_MIB = 12


def dot(a, b):
    return jnp.dot(a, b, preferred_element_type=F32)


def silu_of_half(h):
    return h + h * jnp.tanh(h)


def turned(v, shift):
    shift %= 128
    if shift == 0:
        return v
    return jnp.concatenate([v[:, 128 - shift :], v[:, : 128 - shift]], axis=1)


def widened(row):
    return jnp.concatenate([row, jnp.zeros((row.shape[0], 128 - row.shape[1]), BF)], axis=1)


def with_columns(row, right_ref, left_ref, lead, r):
    per = 128 // SLOT
    cols = row.shape[1]
    at = (r % per) * SLOT
    right = turned(right_ref[lead, r // per], cols - at)
    left = turned(left_ref[lead, r // per], 128 - SLOT - at)
    return jnp.concatenate([row, right[:, cols : cols + SLOT], left[:, cols + SLOT :]], axis=1)


def three_taps(row):
    cin = row.shape[0]
    fill = jnp.zeros((256 - 3 * cin, 128), BF)
    tall = jnp.concatenate([row, row, row, fill], axis=0).T
    lane = lax.broadcasted_iota(jnp.int32, (128, 128), 1)
    low, high = tall[:, :128], tall[:, 128:]
    before = jnp.concatenate([low[127:], low[:127]], axis=0)
    after = jnp.concatenate([high[1:], high[:1]], axis=0)
    low = jnp.where(lane < cin, before, low)
    high = jnp.where(lane < 2 * cin - 128, high, after)
    return jnp.concatenate([low, high], axis=1)


def pack_columns(*refs):
    *x_refs, west_ref, east_ref, choice = refs
    per = 128 // SLOT
    offset = x_refs[0].shape[3] - SLOT

    @pl.when(pl.program_id(0) == 0)
    def _():
        source = lax.broadcasted_iota(jnp.int32, (128, 256), 0)
        target = lax.broadcasted_iota(jnp.int32, (128, 256), 1)
        is_east = target >= 128
        lane = jnp.where(is_east, target - 128, target)
        wanted = jnp.where(is_east, offset, 0) + lax.rem(lane, SLOT)
        same = source == wanted
        spot = lane // SLOT
        for i in range(per):
            keep = jnp.where(same & (spot == i), 1.0, 0.0)
            choice[i * 128 : i * 128 + 128] = keep.astype(BF)

    lhs = jnp.concatenate(
        [
            jnp.concatenate([widened(x_ref[0, i]) for i in range(per)], axis=1)
            for x_ref in x_refs
        ],
        axis=0,
    )
    packed = dot(lhs, choice[...]).astype(BF)
    cin = x_refs[0].shape[2]
    for group in range(len(x_refs)):
        rows = slice(group * cin, group * cin + cin)
        west_ref[0, group] = packed[rows, :128]
        east_ref[0, group] = packed[rows, 128:]


def make_near(lift_ref, near_ref, wn_ref):
    cin, chan = lift_ref.shape
    wn_ref[...] = jnp.zeros_like(wn_ref)
    for a in range(3):
        for b in range(3):
            near = (0.5 * dot(lift_ref[...], near_ref[a, b])).astype(BF)
            for o in range(2):
                wn_ref[a + o, b * cin : (b + 1) * cin, o * chan : (o + 1) * chan] = near


def make_far(far_ref, mix_ref, wf_ref, wm_ref):
    chan = mix_ref.shape[0]
    wf_ref[...] = jnp.zeros_like(wf_ref)
    wm_ref[...] = jnp.zeros_like(wm_ref)
    for a in range(3):
        for b in range(3):
            far = (0.5 * far_ref[a, b].astype(F32)).astype(BF)
            for o in range(2):
                k = a + o
                base = (2 * b + k // 2) * 256 + (k % 2) * chan
                wf_ref[base : base + chan, o * chan : (o + 1) * chan] = far
    wm_ref[:chan, :chan] = mix_ref[...]
    wm_ref[chan:, chan:] = mix_ref[...]


def pack_rows(rows, top_ref, bottom_ref, right_ref, left_ref, p_ref, q_ref):
    even = lax.rem(lax.axis_index("lat"), 2) == 0
    top, bottom = [], []
    for k in range(HALO):
        top.append(with_columns(top_ref[0, k], right_ref, left_ref, 0, k))
        r = rows - HALO + k
        bottom.append(with_columns(bottom_ref[0, 8 - HALO + k], right_ref, left_ref, 0, r))
    for k in range(HALO):
        p_ref[0, k] = jnp.where(even, top[k], bottom[k])
        q_ref[0, k] = jnp.where(even, bottom[k], top[k])


def past_edges(piece):
    return jnp.concatenate([piece[128 - FAR :], piece[: 128 - FAR]], axis=0)


def place(f2, at, half, piece):
    f2[(*at, slice(None), slice(half * 128, half * 128 + 128))] = piece


def tap(ref, b, at, c):
    cols = ref.shape[-2] - 16
    return ref[(*at, c, slice(b * FAR, b * FAR + cols))]


def near_block(rows, wn_ref):
    lhs = jnp.concatenate(
        [jnp.concatenate([pair[i] for pair in rows], axis=0) for i in range(4)], axis=1
    )
    return silu_of_half(dot(lhs, wn_ref[...].reshape(4 * 256, 256)))


def far_block(uppers, lowers, wf_ref):
    lhs = jnp.concatenate(
        [
            jnp.concatenate([tap(ref, b, at, c) for ref, at in refs for c in range(4)], axis=0)
            for b in range(3)
            for refs in (uppers, lowers)
        ],
        axis=1,
    )
    return silu_of_half(dot(lhs, wf_ref[...])).astype(BF)


def halves(v, pair, height):
    base = height * pair
    return [v[base : base + height, 128 * o : 128 * o + 128] for o in range(2)]


def first_rows(
    x_ref, lift_ref, near_ref, far_ref, mix_ref, first_ref, wn_ref, wf_ref, wm_ref, *x3s
):

    @pl.when(pl.program_id(0) == 0)
    def _():
        make_near(lift_ref, near_ref, wn_ref)
        make_far(far_ref, mix_ref, wf_ref, wm_ref)

    cols = x_ref.shape[3]
    blocks = first_ref.shape[1]

    def build(m):
        for i in range(2 if m else 0, 10):
            taps = three_taps(widened(x_ref[0, 8 * m + i + FAR - 1]))[:cols]
            x3s[m][i] = taps
            if i >= 8 and m + 1 < blocks:
                x3s[m + 1][i - 8] = taps

    def store(m, v):
        for p in range(4):
            for o, piece in enumerate(halves(v, p, cols)):
                h, c = divmod(2 * p + o, 4)
                first_ref[0, m, h, c] = piece

    build(0)
    for m in range(blocks):
        rows = [[x3s[m][2 * p + i] for i in range(4)] for p in range(4)]
        if m + 1 < blocks:
            build(m + 1)
        store(m, near_block(rows, wn_ref).astype(BF))


def joined(main, strip):
    end = main.shape[0]
    head = jnp.concatenate([strip[14:15], main[:16].astype(F32)[1:]], axis=0)
    tail = jnp.concatenate([main[end - 16 :].astype(F32)[:15], strip[1:2]], axis=0)
    beyond = jnp.concatenate([strip[2:6], strip[2:10], strip[10:14]], axis=0)
    return jnp.concatenate(
        [head.astype(BF), main[16 : end - 16], tail.astype(BF), beyond.astype(BF)], axis=0
    )


def build_strips(b, west_ref, east_ref, right_ref, left_ref, strips):
    cin = west_ref.shape[2]
    per = 128 // SLOT
    lane = lax.rem(lax.broadcasted_iota(jnp.int32, (cin, 128), 1), SLOT)
    for g in range(west_ref.shape[1]):
        right = jnp.where(lane < 2, turned(east_ref[b, g], -6), turned(right_ref[b, g], 2))
        left = jnp.where(lane < 6, turned(left_ref[b, g], -2), turned(west_ref[b, g], 6))
        right, left = three_taps(right), three_taps(left)
        for i in range(per):
            at = slice(SLOT * i, SLOT * i + SLOT)
            strips[per * g + i] = jnp.concatenate([right[at], left[at]], axis=0)


def inner_rows(
    first_ref, west_ref, east_ref, right_ref, left_ref, wn_ref, wf_ref, wm_ref,
    out_ref, fx_ref, edge, s, *scratch,
):
    batch = west_ref.shape[0]
    strips, f2s = scratch[:batch], scratch[batch:]
    blocks = len(f2s)
    cols = f2s[0].shape[-2] - 16
    pairs = 4 * blocks

    @pl.when(pl.program_id(0) == 0)
    def _():
        for b in range(batch + 1):
            if b < batch:
                build_strips(b, west_ref, east_ref, right_ref, left_ref, strips[b])
            if b > 0:
                rows = [
                    [strips[b - 1][FAR - 1 + 2 * q + i] for i in range(4)] for q in range(pairs)
                ]
                edge[b - 1] = near_block(rows, wn_ref)

    sample = pl.program_id(0)
    span = 4 * cols

    def far(g):
        near, next_ = ([(f2s[i + k], ()) for i in range(g, g + WIDE)] for k in range(2))
        s[g * span : (g + WIDE) * span] = far_block(near, next_, wf_ref)

    for m in range(blocks):
        for p in range(4):
            q = 4 * m + p
            for o, strip in enumerate(halves(edge[sample, 16 * q : 16 * q + 16], 0, 16)):
                h, c = divmod(2 * p + o, 4)
                piece = past_edges(joined(first_ref[0, m, h, c], strip))
                place(f2s[m], (c,), h, piece)
                if m == 0:
                    fx_ref[0, 0, h, c] = piece
                if m == blocks - 1:
                    fx_ref[0, 1, h, c] = piece
        if m >= WIDE and (m - WIDE) % WIDE == 0:
            far(m - WIDE)
    y = dot(s[...], wm_ref[...]).astype(BF)
    for g in range(blocks - 1):
        for c in range(4):
            at = g * span + c * cols
            for h in range(2):
                out_ref[0, 8 * g + 4 * h + c] = y[at : at + cols, 128 * h : 128 * h + 128]


def outer_rows(
    p_own_ref, q_own_ref, p_ref, q_ref, fx_ref,
    wn_ref, wf_ref, wm_ref, _, out_ref, s, y, sems, *scratch,
):
    lat = lax.axis_index("lat")
    even = lax.rem(lat, 2) == 0
    poles = (lat == 0, lat == lax.axis_size("lat") - 1)
    units = [(b, side) for b in range(p_ref.shape[0]) for side in range(2)]
    count = len(units)
    x3s, f2s = scratch[:count], scratch[count:]
    cols = f2s[0].shape[-2] - 16
    total = out_ref.shape[1]
    span = 4 * cols

    def build(u):
        b, side = units[u]
        x3 = x3s[u]
        pole = poles[side]
        moved = pole if side == 0 else jnp.logical_not(pole)
        from_p = even if side == 0 else jnp.logical_not(even)
        base = jnp.where(moved, 1, 0)
        close = jnp.where(moved, 0, HALO - 1)
        for k in range(HALO):
            x3[base + k] = three_taps(jnp.where(from_p, p_ref[b, k], q_ref[b, k]))
        x3[6 if side == 0 else 11] = x3[base + close]
        for k in range(HALO):
            taps = three_taps(jnp.where(from_p, p_own_ref[b, k], q_own_ref[b, k]))
            x3[(7 if side == 0 else 6) + k] = taps
            if k == (0 if side == 0 else HALO - 1):
                x3[jnp.where(moved, 0, HALO)] = taps

    def first(u):
        b, side = units[u]
        pole = poles[side]
        rows = [[x3s[u][at + i] for i in range(4)] for at in (0, 2, 6, 8)]
        v = near_block(rows, wn_ref).astype(BF)
        for q in range(2):
            for o, piece in enumerate(halves(v, q, 128)):
                c = 2 * q + o
                row = jnp.where(pole, 3 - c, c)
                place(f2s[u], (side, row), side, past_edges(piece))
            for o, piece in enumerate(halves(v, 2 + q, 128)):
                place(f2s[u], (side, 2 * q + o), 1 - side, past_edges(piece))

    def known(u):
        b, side = units[u]
        for h in range(2):
            for c in range(4):
                place(f2s[u], (1 - side, c), h, fx_ref[b, side, h, c])

    copies = []

    def finish(u):
        b, side = units[u]
        done = dot(s[u * span : (u + 1) * span], wm_ref[...]).astype(BF)
        for c in range(4):
            for h in range(2):
                y[u, 4 * h + c] = done[cols * c : cols * c + cols, 128 * h : 128 * h + 128]
        to = out_ref.at[b, pl.ds(0 if side == 0 else total - 8, 8)]
        copy = pltpu.make_async_copy(y.at[u], to, sems.at[u])
        copy.start()
        copies.append(copy)

    build(0)
    for u in range(count):
        if u + 1 < count:
            build(u + 1)
        known(u)
        first(u)
    for u in range(count):
        s[u * span : (u + 1) * span] = far_block([(f2s[u], (0,))], [(f2s[u], (1,))], wf_ref)
        if (u + 1) % EVERY == 0:
            for done_unit in range(u + 1 - EVERY, u + 1):
                finish(done_unit)
    for copy in copies:
        copy.wait()


def whole(shape):
    return pl.BlockSpec(shape, lambda *_: (0,) * len(shape))


def per_sample(shape):
    return pl.BlockSpec((1,) + shape[1:], lambda b, *_: (b,) + (0,) * (len(shape) - 1))


def params(mib):
    return pltpu.CompilerParams(vmem_limit_bytes=mib * MIB)


def cost(flops, nbytes):
    return pl.CostEstimate(flops=flops, bytes_accessed=nbytes, transcendentals=0)


def swaps(lats, lons, offset):
    half = lons // 2
    pairs = []
    for lat in range(lats):
        other = lat + (1 if (lat + offset) % 2 == 0 else -1)
        for lon in range(lons):
            if 0 <= other < lats:
                pairs.append((lon * lats + other, lon * lats + lat))
            else:
                pairs.append(((lon + half) % lons * lats + lat, lon * lats + lat))
    return pairs


def edge_shape(x):
    per = 128 // SLOT
    return (x.shape[0], -(-x.shape[1] // per), x.shape[2], 128)


def call_pack(x):
    edge = edge_shape(x)
    return pl.pallas_call(
        pack_columns,
        grid=(x.shape[0],),
        in_specs=[
            pl.BlockSpec(
                (1, 128 // SLOT, x.shape[2], x.shape[3]), functools.partial(lambda g, b: (b, g, 0, 0), g)
            )
            for g in range(edge[1])
        ],
        out_specs=[per_sample(edge)] * 2,
        out_shape=[jax.ShapeDtypeStruct(edge, BF)] * 2,
        scratch_shapes=[pltpu.VMEM((128 * 128 // SLOT, 256), BF)],
        compiler_params=params(PACK_MIB),
        cost_estimate=cost(0, 4 * MIB),
        name="pack_columns",
    )(*[x] * edge[1])


def call_first(x, weights):
    batch, rows, _, cols = x.shape
    chan = weights[-1].shape[1]
    first = (batch, rows // 8 - 1, 2, 4, cols, chan)
    return pl.pallas_call(
        first_rows,
        grid=(batch,),
        in_specs=[per_sample(x.shape)] + [whole(w.shape) for w in weights],
        out_specs=[per_sample(first)] + [whole(shape) for shape in MADE],
        out_shape=[jax.ShapeDtypeStruct(shape, BF) for shape in (first, *MADE)],
        scratch_shapes=[pltpu.VMEM((10, cols, 256), BF)] * (rows // 8 - 1),
        compiler_params=params(FIRST_MIB),
        cost_estimate=cost(6 * 10**9, 9 * MIB),
        name="first_rows",
    )(x, *weights)


def call_inner(first, west, east, right, left, made, rows):
    batch, blocks, _, _, cols, chan = first.shape
    fx = (batch, 2, 2, 4, 128, chan)
    inner = rows - 16
    return pl.pallas_call(
        inner_rows,
        grid=(batch,),
        in_specs=[per_sample(first.shape)]
        + [whole(right.shape)] * 4
        + [whole(shape) for shape in MADE],
        out_specs=[
            pl.BlockSpec(
                (pl.Element(1), pl.Element(inner), pl.Element(cols), pl.Element(chan)),
                lambda b: (b, 8, 0, 0),
            ),
            per_sample(fx),
        ],
        out_shape=[
            jax.ShapeDtypeStruct(shape, BF)
            for shape in ((batch, rows, cols, chan), fx)
        ],
        scratch_shapes=[
            pltpu.VMEM((batch, 16 * 4 * blocks, 256), F32),
            pltpu.VMEM(((blocks - 1) * 4 * cols, 256), BF),
        ]
        + [pltpu.VMEM((rows, 16, 256), BF)] * batch
        + [pltpu.VMEM((4, cols + 16, 256), BF)] * blocks,
        compiler_params=params(INNER_MIB),
        cost_estimate=cost(7 * 10**9, 12 * MIB),
        name="inner_rows",
    )(first, west, east, right, left, *made)


def on_device(fields, lift_weight, near_kernel, far_kernel, mix_weight):
    batch, rows, cols, cin = fields.shape
    chan = mix_weight.shape[1]
    lats, lons = lax.axis_size("lat"), lax.axis_size("lon")
    x = jnp.transpose(fields, (0, 1, 3, 2))
    edge = edge_shape(x)
    west, east = call_pack(x)
    right = lax.ppermute(west, "lon", [((i + 1) % lons, i) for i in range(lons)])
    left = lax.ppermute(east, "lon", [((i - 1) % lons, i) for i in range(lons)])
    weights = (lift_weight, near_kernel, far_kernel, mix_weight)
    first, *made = call_first(x, weights)
    strip = (batch, HALO, cin, 128)
    last = rows // 8 - 1
    p_send, q_send = pl.pallas_call(
        functools.partial(pack_rows, rows),
        grid=(batch,),
        in_specs=[
            pl.BlockSpec((1, 8, cin, cols), lambda b: (b, 0, 0, 0)),
            pl.BlockSpec((1, 8, cin, cols), lambda b: (b, last, 0, 0)),
            per_sample(edge),
            per_sample(edge),
        ],
        out_specs=[per_sample(strip)] * 2,
        out_shape=[jax.ShapeDtypeStruct(strip, BF)] * 2,
        compiler_params=params(PACK_MIB),
        cost_estimate=cost(0, 2 * MIB),
        name="pack_rows",
    )(x, x, right, left)
    p_got = lax.ppermute(p_send, ("lon", "lat"), swaps(lats, lons, 1))
    q_got = lax.ppermute(q_send, ("lon", "lat"), swaps(lats, lons, 0))

    out, edges = call_inner(first, west, east, right, left, made, rows)
    units = 2 * batch
    fx = edges.shape
    return pl.pallas_call(
        outer_rows,
        grid=(1,),
        in_specs=[whole(strip)] * 4
        + [whole(fx)]
        + [whole(shape) for shape in MADE]
        + [pl.BlockSpec(memory_space=pl.ANY)],
        out_specs=pl.BlockSpec(memory_space=pl.ANY),
        out_shape=jax.ShapeDtypeStruct((batch, rows, cols, chan), BF),
        scratch_shapes=[
            pltpu.VMEM((units * 4 * cols, 256), BF),
            pltpu.VMEM((units, 8, cols, chan), BF),
            pltpu.SemaphoreType.DMA((units,)),
        ]
        + [pltpu.VMEM((12, 128, 256), BF)] * units
        + [pltpu.VMEM((2, 4, cols + 16, 256), BF)] * units,
        input_output_aliases={8: 0},
        compiler_params=params(OUTER_MIB),
        cost_estimate=cost(5 * 10**9, 6 * MIB),
        name="outer_rows",
    )(p_send, q_send, p_got, q_got, edges, *made, out)


def solution(mesh):
    return jax.shard_map(
        on_device,
        mesh=mesh,
        in_specs=(P(None, "lat", "lon", None), P(), P(), P(), P()),
        out_specs=P(None, "lat", "lon", None),
        check_vma=False,
    )
```
